32 devices in a mesh: dp: 4 (over z), label: 8 (over y, x, core).
Axes of the slice: x: 2, y: 2, z: 4, core: 2. Of those that a mesh axis runs over, the one named last changes fastest.
Arguments:
- queries: bfloat16 [4096, 1024], P(('dp', 'label')), may hold values from -6 to 6
- beams: int32 [4096, 20], P(('dp', 'label')), may hold values from 0 to 255, all different within a row; in each aligned block of 128 rows (0 to 127, 128 to 255, ...) at most 12 rows name the same one
- positive_slots: int32 [4096, 4], P(('dp', 'label')), may hold values from 0 to 2559
- owner: int32 [256], replicated, may hold values from 0 to 255, each once
- label_weight: bfloat16 [32768, 1024], P('label'), may hold values from -0.1875 to 0.1875
Outputs:
- query_grad: float32 [4096, 1024], P(('dp', 'label'))
- new_weight: float32 [32768, 1024], P(('label', 'dp'))
The draws below stay inside these ranges and needn't reach their ends.
Inputs may be any that keep to these rules, and one draw needn't show every extreme that they name: `beams`: among the 128 rows of one device (aligned blocks of rows), no cluster is named by more than 12 rows, a bound that some block reaches; a row names 20 different clusters. `positive_slots`: position v stands for label v mod 128 of beam entry v // 128; repeats may occur. `owner`: each block of rows is named once.
All inputs are finite; a program needn't handle non-finite values.
Results may differ from the reference program's by a relative error of at most 0.0035.
Values may be sent and summed in bfloat16 or wider, within the bound.
A program may use at most 128 MiB of HBM per device.

```python
import math
import jax
import jax.numpy as jnp
import numpy as np
from jax import lax

D = 1024
CL = 128
K = 20
P_SIZE = 4
CLUSTERS = 256
Q_DEV = 128
MOST = 12
QUERIES = 4096
N_DP = 4
N_LABEL = 8


def touch_ends(drawn, rng, low, top_value):
    extent = drawn.shape
    index_at = [jax.random.randint(jax.random.fold_in(rng, axis), (), 0, extent[axis]) for axis in range(len(extent))]
    drawn = drawn.at[tuple(index_at)].set(low)
    longest = extent.index(max(extent))
    index_at[longest] = (index_at[longest] + 1) % extent[longest]
    return drawn.at[tuple(index_at)].set(top_value)


def shard_levels(stream_key, shape, cuts, least, high):
    level = 1.0
    for axis_at, shards_of in cuts:
        steps = jax.random.uniform(jax.random.fold_in(jax.random.fold_in(stream_key, 6), axis_at), (shards_of,), jnp.float32, least / len(cuts), high / len(cuts))
        level = level * jnp.repeat(jnp.exp(steps), shape[axis_at] // shards_of).reshape((-1,) + (1,) * (len(shape) - 1 - axis_at))
    return level


def shared_out(stream_key, own, number, rows, number_of, top, most, slope):
    sequence = jax.random.permutation(stream_key, number_of)
    packed, ordinary = portions_of(number_of, rows * top, most, slope, True), portions_of(number_of, rows * top, most, slope, False)
    places = jnp.arange(number_of)

    def named(tallies, rotation):
        used = int((tallies > 0).sum())
        fixed = max(1, used // 4)
        moved = fixed + (places - fixed + rotation * (used - fixed)) % max(1, number_of - fixed)
        return jnp.zeros((number_of,), jnp.int32).at[sequence[jnp.where(places < fixed, places, moved)]].set(jnp.asarray(tallies, jnp.int32))

    tallies = jnp.where(number % 4 == 0, named(packed, number // 4), named(ordinary, number - number // 4 - 1))
    mixed = jax.random.permutation(jax.random.fold_in(own, 3), number_of)
    donor, receiver = mixed[0:number_of // 2 * 2:2], mixed[1:number_of // 2 * 2:2]
    slack = jnp.minimum(tallies[donor] - 1, most - tallies[receiver]) // 2
    slack = jnp.where((donor == sequence[0]) | (receiver == sequence[0]) | (tallies[receiver] == 0), 0, jnp.maximum(slack, 0))
    moved = jax.random.randint(jax.random.fold_in(own, 4), (number_of // 2,), 0, 1 << 20) % (slack + 1)
    tallies = tallies.at[donor].add(-moved).at[receiver].add(moved)
    members = jnp.searchsorted(jnp.cumsum(tallies), jnp.arange(rows * top), side="right").astype(jnp.int32)
    table = members.reshape(top, rows).T
    table = table[jax.random.permutation(jax.random.fold_in(own, 1), rows)]
    rotation = jax.random.randint(jax.random.fold_in(own, 2), (rows, 1), 0, top)
    return jnp.take_along_axis(table, (jnp.arange(top)[None, :] + rotation) % top, axis=1)


def portions_of(amount, total, bound, lean, full):
    weights = [(1 << 20) // math.isqrt(rank ** lean) + 1 for rank in range(1, amount + 1)]
    largest = bound if full else min(bound, max(-(-total // amount), total * weights[0] // sum(weights)))
    least = 1 if total - largest >= amount - 1 else 0
    given, surplus = [largest] + [least] * (amount - 1), total - largest - least * (amount - 1)
    while surplus > 0:
        free = [i for i in range(1, amount) if given[i] < largest] or [i for i in range(1, amount) if given[i] < bound]
        mass, left = sum([weights[i] for i in free]), surplus
        for i in free:
            extra = min(bound - given[i], max(1, left * weights[i] // mass), surplus)
            given[i] = given[i] + extra
            surplus = surplus - extra
    return np.array(given)


def centred(stream_key, dims, scale, bound, split=(), kind=jnp.bfloat16):
    drawn = scale * jax.random.normal(stream_key, dims, jnp.float32)
    if split:
        drawn = drawn * shard_levels(stream_key, dims, split, -0.22, 0.18)
    return jnp.clip(drawn, -bound, bound).astype(kind)


def setup_inputs(seed: int = 0) -> dict:
    streams_of = jax.random.split(jax.random.key(seed), 6)
    queries = centred(streams_of[0], (QUERIES, D), 1.0, 6.0, ((0, 32),))
    beams_keys = jax.random.split(jax.random.fold_in(streams_of[1], 1), QUERIES // Q_DEV)
    beams_turns = jax.random.permutation(jax.random.fold_in(streams_of[1], 3), QUERIES // Q_DEV)
    beams = jax.vmap(lambda own, number: shared_out(jax.random.fold_in(streams_of[1], 2), own, number, Q_DEV, CLUSTERS, K, MOST, 1))(beams_keys, beams_turns).reshape((QUERIES, K))
    positive_slots = touch_ends(jax.random.randint(streams_of[2], (QUERIES, P_SIZE), 0, K * CL), jax.random.fold_in(streams_of[2], 1), 0, (K * CL) - 1).astype(jnp.int32)
    owner = jax.random.permutation(streams_of[3], CLUSTERS).astype(jnp.int32)
    label_weight = centred(streams_of[4], (CLUSTERS * CL, D), D ** -0.5, 0.1875, ((0, 8),))
    return dict(queries=queries, beams=beams, positive_slots=positive_slots, owner=owner, label_weight=label_weight)


STEP_SIZE = 0.02


def reference(queries, beams, positive_slots, owner, label_weight):
    total_pairs = QUERIES * K
    capacity = N_DP * N_LABEL * MOST
    flat_beams = beams.reshape(-1)
    pair_ids = jnp.arange(total_pairs, dtype=jnp.int32)
    inverse = jnp.zeros((CLUSTERS,), jnp.int32).at[owner].set(jnp.arange(CLUSTERS, dtype=jnp.int32))
    blocks = label_weight.reshape(CLUSTERS, CL, D)
    padded = jnp.concatenate([queries, jnp.zeros((1, D), queries.dtype)], axis=0)
    labels = jnp.arange(CL, dtype=jnp.int32)

    def one_slot(grads, slot):
        cluster = inverse[slot]
        hit = (flat_beams == cluster).astype(jnp.int32)
        order = jnp.cumsum(hit) - 1
        target = jnp.where(hit > 0, order, capacity).astype(jnp.int32)
        rows = jnp.full((capacity,), total_pairs, jnp.int32).at[target].set(pair_ids, mode="drop")
        live = rows < total_pairs
        query_row = jnp.where(live, rows // K, QUERIES).astype(jnp.int32)
        column = (rows % K).astype(jnp.int32)
        weights = lax.dynamic_index_in_dim(blocks, slot, 0, keepdims=False)
        picked = padded[query_row]
        scores = jnp.dot(picked, weights.T, preferred_element_type=jnp.float32)
        offsets = positive_slots[jnp.minimum(query_row, QUERIES - 1)]
        wanted = column[:, None, None] * CL + labels[None, None, :]
        positive = jnp.any(offsets[:, :, None] == wanted, axis=1).astype(jnp.float32)
        signal = ((jax.nn.sigmoid(scores) - positive) * live[:, None].astype(jnp.float32)).astype(jnp.bfloat16)
        block_grad = jnp.dot(signal.T, picked, preferred_element_type=jnp.float32)
        partial_rows = jnp.dot(signal, weights, preferred_element_type=jnp.float32).astype(jnp.bfloat16)
        partial_rows = lax.optimization_barrier(partial_rows).astype(jnp.float32)
        grads = grads.at[query_row].add(partial_rows, mode="drop")
        return grads, block_grad

    start = jnp.zeros((QUERIES, D), jnp.float32)
    grads, block_grads = lax.scan(one_slot, start, jnp.arange(CLUSTERS, dtype=jnp.int32))
    new_weight = label_weight.astype(jnp.float32) - STEP_SIZE * block_grads.reshape(CLUSTERS * CL, D)
    return grads, new_weight
```

```python
import jax
import jax.numpy as jnp
from jax import lax
from jax.sharding import PartitionSpec as P

STEP_SIZE = 0.02


def slot_table(keys, count, most):
    q_rows, beam = keys.shape
    pairs = q_rows * beam
    ids = jnp.arange(count, dtype=jnp.int32)
    member = jnp.any(keys[:, :, None] == ids[None, None, :], axis=1).astype(jnp.float32)
    row_ids = jnp.arange(q_rows, dtype=jnp.int32)
    lower = (row_ids[:, None] > row_ids[None, :]).astype(jnp.float32)
    before = jnp.dot(lower, member, precision=lax.Precision.HIGHEST)
    safe_keys = jnp.minimum(keys, count - 1)
    rank = jnp.take_along_axis(before, safe_keys, axis=1).astype(jnp.int32)
    flat_keys = keys.reshape(pairs)
    target = jnp.where(flat_keys < count, flat_keys * most + rank.reshape(pairs), count * most)
    table = (
        jnp.full((count * most,), pairs, jnp.int32)
        .at[target]
        .set(jnp.arange(pairs, dtype=jnp.int32), mode="drop")
    )
    return (target, table)


def body(queries, beams, positive_slots, owner, label_weight):
    n_label = lax.axis_size("label")
    q_dev, width = queries.shape
    beam = beams.shape[1]
    n_pos = positive_slots.shape[1]
    clusters = owner.shape[0]
    clus_dev = clusters // n_label
    cluster_size = label_weight.shape[0] // clus_dev
    most = max(2, q_dev * 3 // 32)
    pairs = q_dev * beam
    rows_dev = clus_dev * most
    lookup = beams[:, :, None] == jnp.arange(clusters, dtype=jnp.int32)[None, None, :]
    pair_slot = jnp.sum(jnp.where(lookup, owner[None, None, :], 0), axis=2)
    position = jnp.arange(beam, dtype=jnp.int32)
    inside = positive_slots[:, None, :] // cluster_size == position[None, :, None]
    pair_offset = jnp.where(inside, positive_slots[:, None, :] % cluster_size, -1)
    target, table = slot_table(pair_slot, clusters, most)
    filled = table < pairs
    padded = jnp.concatenate([queries, jnp.zeros((1, width), queries.dtype)], axis=0)
    send_q = padded[jnp.where(filled, table // beam, q_dev)]
    flat_off = pair_offset.reshape(pairs, n_pos)
    send_off = jnp.where(filled[:, None], flat_off[jnp.where(filled, table, 0)], -1)
    moved = (
        lax.all_to_all(
            send_q.reshape(n_label, rows_dev, width),
            "label",
            split_axis=0,
            concat_axis=0,
            tiled=True,
        ),
        lax.all_to_all(
            send_off.astype(jnp.bfloat16).reshape(n_label, rows_dev, n_pos),
            "label",
            split_axis=0,
            concat_axis=0,
            tiled=True,
        ),
        lax.all_to_all(
            filled.astype(jnp.bfloat16).reshape(n_label, rows_dev),
            "label",
            split_axis=0,
            concat_axis=0,
            tiled=True,
        ),
    )
    recv_q = moved[0]
    recv_off = moved[1].astype(jnp.int32)
    recv_fill = moved[2].astype(jnp.float32)
    incoming = n_label * most
    recv_q = (
        recv_q.reshape(n_label, clus_dev, most, width)
        .transpose(1, 0, 2, 3)
        .reshape(clus_dev, incoming, width)
    )
    recv_off = (
        recv_off.reshape(n_label, clus_dev, most, n_pos)
        .transpose(1, 0, 2, 3)
        .reshape(clus_dev, incoming, n_pos)
    )
    recv_fill = (
        recv_fill.reshape(n_label, clus_dev, most).transpose(1, 0, 2).reshape(clus_dev, incoming)
    )
    weights = label_weight.reshape(clus_dev, cluster_size, width)
    scores = jnp.einsum("cnd,cld->cnl", recv_q, weights, preferred_element_type=jnp.float32)
    labels = jnp.arange(cluster_size, dtype=jnp.int32)
    positive = jnp.any(recv_off[..., None] == labels, axis=-2).astype(jnp.float32)
    signal = ((jax.nn.sigmoid(scores) - positive) * recv_fill[..., None]).astype(jnp.bfloat16)
    signal_split = signal.reshape(clus_dev, n_label, most, cluster_size)
    part_dq = jnp.einsum(
        "csml,cld->scmd", signal_split, weights, preferred_element_type=jnp.float32
    ).astype(jnp.bfloat16)
    part_dw = jnp.einsum("cnl,cnd->cld", signal, recv_q, preferred_element_type=jnp.float32)
    part_dw = part_dw.reshape(clus_dev * cluster_size, width)
    back = lax.all_to_all(
        part_dq.reshape(n_label, rows_dev, width), "label", split_axis=0, concat_axis=0, tiled=True
    )
    back_rows = back.reshape(clusters * most, width)[target]
    query_grad = jnp.sum(back_rows.reshape(q_dev, beam, width).astype(jnp.float32), axis=1)
    summed = lax.psum_scatter(part_dw, "dp", scatter_dimension=0, tiled=True)
    share = summed.shape[0]
    own_rows = lax.dynamic_slice_in_dim(
        label_weight, lax.axis_index("dp") * share, share, 0
    ).astype(jnp.float32)
    return (query_grad, own_rows - STEP_SIZE * summed)


def dense_body(queries, beams, positive_slots, owner, label_weight):
    n_label = lax.axis_size("label")
    n_dp = lax.axis_size("dp")
    q_dev, width = queries.shape
    beam = beams.shape[1]
    n_pos = positive_slots.shape[1]
    clusters = owner.shape[0]
    clus_dev = clusters // n_label
    cluster_size = label_weight.shape[0] // clus_dev
    rows_dev = label_weight.shape[0]
    share = rows_dev // n_dp
    clus_own = clus_dev // n_dp
    group = q_dev * n_label
    d, l = lax.axis_index("dp"), lax.axis_index("label")
    lookup = beams[:, :, None] == jnp.arange(clusters, dtype=jnp.int32)[None, None, :]
    slot = jnp.sum(jnp.where(lookup, owner[None, None, :], 0), axis=2)
    where_p = positive_slots[:, :, None] // cluster_size == jnp.arange(beam, dtype=jnp.int32)
    pos_slot = jnp.sum(jnp.where(where_p, slot[:, None, :], 0), axis=2)
    pos_label = positive_slots % cluster_size
    meta = jnp.concatenate([slot, pos_slot, pos_label], axis=1).astype(jnp.bfloat16)
    q_all = lax.all_gather(queries, ("dp", "label"), axis=0, tiled=True)
    m_all = lax.all_gather(meta, ("dp", "label"), axis=0, tiled=True).astype(jnp.int32)

    def signal_of(q, m, w, first, count):
        scores = jnp.dot(q, w.T, preferred_element_type=jnp.float32)
        ids = first + jnp.arange(count, dtype=jnp.int32)
        member = jnp.any(m[:, :beam, None] == ids, axis=1)
        rows = first * cluster_size + jnp.arange(count * cluster_size, dtype=jnp.int32)
        pos = m[:, beam:beam + n_pos] * cluster_size + m[:, beam + n_pos:]
        hit = jnp.any(pos[:, :, None] == rows, axis=1).astype(jnp.float32)
        member = jnp.repeat(member, cluster_size, axis=1)
        return jnp.where(member, jax.nn.sigmoid(scores) - hit, 0.0).astype(jnp.bfloat16)

    q_grp = lax.dynamic_slice_in_dim(q_all, d * group, group, 0)
    m_grp = lax.dynamic_slice_in_dim(m_all, d * group, group, 0)
    sig = signal_of(q_grp, m_grp, label_weight, l * clus_dev, clus_dev)
    part = jnp.dot(sig, label_weight, preferred_element_type=jnp.float32).astype(jnp.bfloat16)
    back = lax.all_to_all(
        part.reshape(n_label, q_dev, width), "label", split_axis=0, concat_axis=0, tiled=True
    )
    query_grad = jnp.sum(back.astype(jnp.float32), axis=0)
    w_own = lax.dynamic_slice_in_dim(label_weight, d * share, share, 0)
    sig2 = signal_of(q_all, m_all, w_own, l * clus_dev + d * clus_own, clus_own)
    dw = jnp.einsum("nr,nd->rd", sig2, q_all, preferred_element_type=jnp.float32)
    return (query_grad, w_own.astype(jnp.float32) - STEP_SIZE * dw)


def choose(queries, beams, positive_slots, owner, label_weight):
    devices = lax.axis_size("dp") * lax.axis_size("label")
    whole_clusters = (owner.shape[0] // lax.axis_size("label")) % lax.axis_size("dp") == 0
    fits = queries.size * devices * 2 <= (16 << 20)
    form = dense_body if (fits and whole_clusters) else body
    return form(queries, beams, positive_slots, owner, label_weight)


def solution(mesh):
    in_specs = (
        P(("dp", "label"), None),
        P(("dp", "label"), None),
        P(("dp", "label"), None),
        P(),
        P("label", None),
    )
    out_specs = (P(("dp", "label"), None), P(("label", "dp"), None))
    return jax.shard_map(
        choose, mesh=mesh, in_specs=in_specs, out_specs=out_specs, check_vma=False
    )
```

```python
import functools

import jax
import jax.numpy as jnp
from jax import lax
from jax.experimental import pallas as pl
from jax.experimental.pallas import tpu as pltpu
from jax.sharding import PartitionSpec as P

STEP_SIZE = 0.02


def slot_table(keys, count, most):
    q_rows, beam = keys.shape
    pairs = q_rows * beam
    ids = jnp.arange(count, dtype=jnp.int32)
    member = jnp.any(keys[:, :, None] == ids[None, None, :], axis=1).astype(jnp.float32)
    row_ids = jnp.arange(q_rows, dtype=jnp.int32)
    lower = (row_ids[:, None] > row_ids[None, :]).astype(jnp.float32)
    before = jnp.dot(lower, member, precision=lax.Precision.HIGHEST)
    safe_keys = jnp.minimum(keys, count - 1)
    rank = jnp.take_along_axis(before, safe_keys, axis=1).astype(jnp.int32)
    flat_keys = keys.reshape(pairs)
    target = jnp.where(flat_keys < count, flat_keys * most + rank.reshape(pairs), count * most)
    table = (
        jnp.full((count * most,), pairs, jnp.int32)
        .at[target]
        .set(jnp.arange(pairs, dtype=jnp.int32), mode="drop")
    )
    return (target, table)


def body(queries, beams, positive_slots, owner, label_weight):
    n_label = lax.axis_size("label")
    q_dev, width = queries.shape
    beam = beams.shape[1]
    n_pos = positive_slots.shape[1]
    clusters = owner.shape[0]
    clus_dev = clusters // n_label
    cluster_size = label_weight.shape[0] // clus_dev
    most = max(2, q_dev * 3 // 32)
    pairs = q_dev * beam
    rows_dev = clus_dev * most
    lookup = beams[:, :, None] == jnp.arange(clusters, dtype=jnp.int32)[None, None, :]
    pair_slot = jnp.sum(jnp.where(lookup, owner[None, None, :], 0), axis=2)
    position = jnp.arange(beam, dtype=jnp.int32)
    inside = positive_slots[:, None, :] // cluster_size == position[None, :, None]
    pair_offset = jnp.where(inside, positive_slots[:, None, :] % cluster_size, -1)
    target, table = slot_table(pair_slot, clusters, most)
    filled = table < pairs
    padded = jnp.concatenate([queries, jnp.zeros((1, width), queries.dtype)], axis=0)
    send_q = padded[jnp.where(filled, table // beam, q_dev)]
    flat_off = pair_offset.reshape(pairs, n_pos)
    send_off = jnp.where(filled[:, None], flat_off[jnp.where(filled, table, 0)], -1)
    moved = (
        lax.all_to_all(
            send_q.reshape(n_label, rows_dev, width),
            "label",
            split_axis=0,
            concat_axis=0,
            tiled=True,
        ),
        lax.all_to_all(
            send_off.astype(jnp.bfloat16).reshape(n_label, rows_dev, n_pos),
            "label",
            split_axis=0,
            concat_axis=0,
            tiled=True,
        ),
        lax.all_to_all(
            filled.astype(jnp.bfloat16).reshape(n_label, rows_dev),
            "label",
            split_axis=0,
            concat_axis=0,
            tiled=True,
        ),
    )
    recv_q = moved[0]
    recv_off = moved[1].astype(jnp.int32)
    recv_fill = moved[2].astype(jnp.float32)
    incoming = n_label * most
    recv_q = (
        recv_q.reshape(n_label, clus_dev, most, width)
        .transpose(1, 0, 2, 3)
        .reshape(clus_dev, incoming, width)
    )
    recv_off = (
        recv_off.reshape(n_label, clus_dev, most, n_pos)
        .transpose(1, 0, 2, 3)
        .reshape(clus_dev, incoming, n_pos)
    )
    recv_fill = (
        recv_fill.reshape(n_label, clus_dev, most).transpose(1, 0, 2).reshape(clus_dev, incoming)
    )
    weights = label_weight.reshape(clus_dev, cluster_size, width)
    scores = jnp.einsum("cnd,cld->cnl", recv_q, weights, preferred_element_type=jnp.float32)
    labels = jnp.arange(cluster_size, dtype=jnp.int32)
    positive = jnp.any(recv_off[..., None] == labels, axis=-2).astype(jnp.float32)
    signal = ((jax.nn.sigmoid(scores) - positive) * recv_fill[..., None]).astype(jnp.bfloat16)
    signal_split = signal.reshape(clus_dev, n_label, most, cluster_size)
    part_dq = jnp.einsum(
        "csml,cld->scmd", signal_split, weights, preferred_element_type=jnp.float32
    ).astype(jnp.bfloat16)
    part_dw = jnp.einsum("cnl,cnd->cld", signal, recv_q, preferred_element_type=jnp.float32)
    part_dw = part_dw.reshape(clus_dev * cluster_size, width)
    back = lax.all_to_all(
        part_dq.reshape(n_label, rows_dev, width), "label", split_axis=0, concat_axis=0, tiled=True
    )
    back_rows = back.reshape(clusters * most, width)[target]
    query_grad = jnp.sum(back_rows.reshape(q_dev, beam, width).astype(jnp.float32), axis=1)
    summed = lax.psum_scatter(part_dw, "dp", scatter_dimension=0, tiled=True)
    share = summed.shape[0]
    own_rows = lax.dynamic_slice_in_dim(
        label_weight, lax.axis_index("dp") * share, share, 0
    ).astype(jnp.float32)
    return (query_grad, own_rows - STEP_SIZE * summed)


SLOTS = 16
CHUNK = 8


def tn_dot(a, b):
    return lax.dot_general(a, b, (((0,), (0,)), ((), ())), preferred_element_type=jnp.float32)


def nt_dot(a, b):
    return lax.dot_general(a, b, (((1,), (1,)), ((), ())), preferred_element_type=jnp.float32)


def pick_matrix(meta, beam, first):
    q_dev = meta.shape[1]
    ids = (first + lax.broadcasted_iota(jnp.int32, (CHUNK, q_dev), 0)).astype(jnp.float32)
    member = meta[32:33, :] == ids
    for j in range(1, beam):
        member = member | (meta[32 + j:33 + j, :] == ids)
    member = member.astype(jnp.float32)
    row = lax.broadcasted_iota(jnp.int32, (q_dev, q_dev), 0)
    col = lax.broadcasted_iota(jnp.int32, (q_dev, q_dev), 1)
    upper = (row < col).astype(jnp.float32).astype(jnp.bfloat16)
    rank = jnp.dot(member.astype(jnp.bfloat16), upper, preferred_element_type=jnp.float32)
    code = jnp.where(member > 0, rank, -1.0)
    wide = jnp.broadcast_to(code[:, None, :], (CHUNK, SLOTS, q_dev))
    place = lax.broadcasted_iota(jnp.int32, (CHUNK, SLOTS, q_dev), 1).astype(jnp.float32)
    pick = (wide == place).astype(jnp.float32).reshape(CHUNK * SLOTS, q_dev)
    return pick.astype(jnp.bfloat16)


def gather_chunk(blk_ref, src, b, first, at, beam, x_ref, off_ref):
    q_dev = blk_ref.shape[2]
    tiles = (blk_ref.shape[1] - 64) // q_dev
    meta = blk_ref[src, tiles * q_dev:tiles * q_dev + 64, :]
    pick = pick_matrix(meta.astype(jnp.float32), beam, first)
    q = jnp.concatenate([blk_ref[src, k * q_dev:(k + 1) * q_dev, :] for k in range(tiles)], axis=1)
    rows = jnp.dot(pick, q, preferred_element_type=jnp.float32).astype(jnp.bfloat16)
    here = pl.ds(pl.multiple_of(b * SLOTS, SLOTS), SLOTS)
    x_ref[pl.ds(at, CHUNK), here, :] = rows.reshape(CHUNK, SLOTS, rows.shape[1])
    high = nt_dot(pick, meta[0:16, :])
    low = nt_dot(pick, meta[16:32, :])
    cluster = first + lax.broadcasted_iota(jnp.int32, high.shape, 0) // SLOTS
    off = jnp.where(high == cluster.astype(jnp.float32), low, -1.0)
    off_ref[pl.ds(at, CHUNK), here, :] = off.reshape(CHUNK, SLOTS, 16)
    return pick


def signal_of(x, off, w, n_pos):
    score = nt_dot(x, w)
    label = lax.broadcasted_iota(jnp.int32, score.shape, 1).astype(jnp.float32)
    hit = off[:, 0:1] == label
    for p in range(1, n_pos):
        hit = hit | (off[:, p:p + 1] == label)
    return (jax.nn.sigmoid(score) - hit.astype(jnp.float32)).astype(jnp.bfloat16)


def step_kernel(n_dp, n_label, beam, n_pos, blk_ref, w_ref, part_ref, new_ref,
                x_ref, y_ref, pick_ref, off_ref, sig_ref):
    d, l = lax.axis_index("dp"), lax.axis_index("label")
    clus_dev = w_ref.shape[0]
    chunks = clus_dev // CHUNK
    rows = CHUNK * SLOTS

    @pl.loop(0, n_label)
    def _(b):
        for h in range(chunks):
            pick = gather_chunk(
                blk_ref, d * n_label + b, b, l * clus_dev + h * CHUNK, h * CHUNK, beam, x_ref, off_ref
            )
            pick_ref[b, h * rows:(h + 1) * rows, :] = pick

    @pl.loop(0, clus_dev // 2)
    def _(c2):
        for u in range(2):
            c = c2 * 2 + u
            w = w_ref[c]
            sig = signal_of(x_ref[c], off_ref[c], w, n_pos)
            sig_ref[c] = sig
            y_ref[c] = jnp.dot(sig, w, preferred_element_type=jnp.float32).astype(jnp.bfloat16)

    @pl.loop(0, n_label)
    def _(b):
        here = pl.ds(pl.multiple_of(b * SLOTS, SLOTS), SLOTS)
        y = y_ref[:, here, :].reshape(clus_dev * SLOTS, y_ref.shape[2])
        part_ref[b] = tn_dot(pick_ref[b], y).astype(jnp.bfloat16)

    @pl.loop(0, CHUNK)
    def _(c):
        at = d * CHUNK + c
        new_ref[c] = w_ref[at].astype(jnp.float32) - STEP_SIZE * tn_dot(sig_ref[at], x_ref[at])

    for step in range(1, n_dp):
        other = lax.rem(d + step, n_dp)

        @pl.loop(0, n_label)
        def _(b):
            gather_chunk(
                blk_ref, other * n_label + b, b, l * clus_dev + d * CHUNK, 0, beam, x_ref, off_ref
            )

        @pl.loop(0, CHUNK // 2)
        def _(c2):
            for u in range(2):
                c = c2 * 2 + u
                x = x_ref[c]
                sig = signal_of(x, off_ref[c], w_ref[d * CHUNK + c], n_pos)
                new_ref[c] = new_ref[c] - STEP_SIZE * tn_dot(sig, x)


def make_block(queries, beams, positive_slots, owner, cluster_size):
    q_dev, width = queries.shape
    beam, n_pos = beams.shape[1], positive_slots.shape[1]
    ids = jnp.arange(owner.shape[0], dtype=jnp.int32)
    lookup = beams[:, :, None] == ids[None, None, :]
    slot = jnp.sum(jnp.where(lookup, owner[None, None, :], 0), axis=2)
    where_p = positive_slots[:, :, None] // cluster_size == jnp.arange(beam, dtype=jnp.int32)
    pos_slot = jnp.sum(jnp.where(where_p, slot[:, None, :], 0), axis=2)
    pos_label = positive_slots % cluster_size
    meta = jnp.concatenate(
        [
            jnp.pad(pos_slot, ((0, 0), (0, 16 - n_pos))),
            jnp.pad(pos_label, ((0, 0), (0, 16 - n_pos))),
            jnp.pad(slot, ((0, 0), (0, 32 - beam)), constant_values=-1),
        ],
        axis=1,
    )
    tiles = queries.reshape(q_dev, width // q_dev, q_dev).transpose(1, 0, 2).reshape(width, q_dev)
    return jnp.concatenate([tiles, meta.T.astype(jnp.bfloat16)], axis=0)


def sparse_body(queries, beams, positive_slots, owner, label_weight):
    n_label = lax.axis_size("label")
    n_dp = lax.axis_size("dp")
    q_dev, width = queries.shape
    clus_dev = owner.shape[0] // n_label
    cluster_size = label_weight.shape[0] // clus_dev
    block = make_block(queries, beams, positive_slots, owner, cluster_size)
    blocks = lax.all_gather(block, ("dp", "label"), axis=0, tiled=False)
    slots = n_label * SLOTS
    part, new = pl.pallas_call(
        functools.partial(step_kernel, n_dp, n_label, beams.shape[1], positive_slots.shape[1]),
        out_shape=(
            jax.ShapeDtypeStruct((n_label, q_dev, width), jnp.bfloat16),
            jax.ShapeDtypeStruct((CHUNK, cluster_size, width), jnp.float32),
        ),
        in_specs=[pl.BlockSpec(memory_space=pltpu.VMEM)] * 2,
        out_specs=(pl.BlockSpec(memory_space=pltpu.VMEM),) * 2,
        scratch_shapes=[
            pltpu.VMEM((clus_dev, slots, width), jnp.bfloat16),
            pltpu.VMEM((clus_dev, slots, width), jnp.bfloat16),
            pltpu.VMEM((n_label, clus_dev * SLOTS, q_dev), jnp.bfloat16),
            pltpu.VMEM((clus_dev, slots, 16), jnp.float32),
            pltpu.VMEM((clus_dev, slots, cluster_size), jnp.bfloat16),
        ],
        compiler_params=pltpu.CompilerParams(vmem_limit_bytes=56 << 20),
    )(blocks, label_weight.reshape(clus_dev, cluster_size, width))
    back = lax.all_to_all(part, "label", split_axis=0, concat_axis=0, tiled=True)
    query_grad = jnp.sum(back.astype(jnp.float32), axis=0)
    return (query_grad, new.reshape(CHUNK * cluster_size, width))


def choose(queries, beams, positive_slots, owner, label_weight):
    n_dp, n_label = lax.axis_size("dp"), lax.axis_size("label")
    q_dev, width = queries.shape
    fits = queries.size * n_dp * n_label * 2 <= (8 << 20) and n_label * SLOTS == q_dev
    fits = fits and q_dev == 128 and width % q_dev == 0 and beams.shape[1] <= 32
    fits = fits and owner.shape[0] == n_label * n_dp * CHUNK and positive_slots.shape[1] <= 16
    fits = fits and max(2, q_dev * 3 // 32) <= SLOTS and owner.shape[0] <= 256
    form = sparse_body if fits else body
    return form(queries, beams, positive_slots, owner, label_weight)


def solution(mesh):
    in_specs = (
        P(("dp", "label"), None),
        P(("dp", "label"), None),
        P(("dp", "label"), None),
        P(),
        P("label", None),
    )
    out_specs = (P(("dp", "label"), None), P(("label", "dp"), None))
    return jax.shard_map(
        choose, mesh=mesh, in_specs=in_specs, out_specs=out_specs, check_vma=False
    )
```

```python
import functools

import jax
import jax.numpy as jnp
from jax import lax
from jax.experimental import pallas as pl
from jax.experimental.pallas import tpu as pltpu
from jax.sharding import PartitionSpec as P

STEP_SIZE = 0.02


def slot_table(keys, count, most):
    q_rows, beam = keys.shape
    pairs = q_rows * beam
    ids = jnp.arange(count, dtype=jnp.int32)
    member = jnp.any(keys[:, :, None] == ids[None, None, :], axis=1).astype(jnp.float32)
    row_ids = jnp.arange(q_rows, dtype=jnp.int32)
    lower = (row_ids[:, None] > row_ids[None, :]).astype(jnp.float32)
    before = jnp.dot(lower, member, precision=lax.Precision.HIGHEST)
    safe_keys = jnp.minimum(keys, count - 1)
    rank = jnp.take_along_axis(before, safe_keys, axis=1).astype(jnp.int32)
    flat_keys = keys.reshape(pairs)
    target = jnp.where(flat_keys < count, flat_keys * most + rank.reshape(pairs), count * most)
    table = (
        jnp.full((count * most,), pairs, jnp.int32)
        .at[target]
        .set(jnp.arange(pairs, dtype=jnp.int32), mode="drop")
    )
    return (target, table)


def body(queries, beams, positive_slots, owner, label_weight):
    n_label = lax.axis_size("label")
    q_dev, width = queries.shape
    beam = beams.shape[1]
    n_pos = positive_slots.shape[1]
    clusters = owner.shape[0]
    clus_dev = clusters // n_label
    cluster_size = label_weight.shape[0] // clus_dev
    most = max(2, q_dev * 3 // 32)
    pairs = q_dev * beam
    rows_dev = clus_dev * most
    lookup = beams[:, :, None] == jnp.arange(clusters, dtype=jnp.int32)[None, None, :]
    pair_slot = jnp.sum(jnp.where(lookup, owner[None, None, :], 0), axis=2)
    position = jnp.arange(beam, dtype=jnp.int32)
    inside = positive_slots[:, None, :] // cluster_size == position[None, :, None]
    pair_offset = jnp.where(inside, positive_slots[:, None, :] % cluster_size, -1)
    target, table = slot_table(pair_slot, clusters, most)
    filled = table < pairs
    padded = jnp.concatenate([queries, jnp.zeros((1, width), queries.dtype)], axis=0)
    send_q = padded[jnp.where(filled, table // beam, q_dev)]
    flat_off = pair_offset.reshape(pairs, n_pos)
    send_off = jnp.where(filled[:, None], flat_off[jnp.where(filled, table, 0)], -1)
    moved = (
        lax.all_to_all(
            send_q.reshape(n_label, rows_dev, width),
            "label",
            split_axis=0,
            concat_axis=0,
            tiled=True,
        ),
        lax.all_to_all(
            send_off.astype(jnp.bfloat16).reshape(n_label, rows_dev, n_pos),
            "label",
            split_axis=0,
            concat_axis=0,
            tiled=True,
        ),
        lax.all_to_all(
            filled.astype(jnp.bfloat16).reshape(n_label, rows_dev),
            "label",
            split_axis=0,
            concat_axis=0,
            tiled=True,
        ),
    )
    recv_q = moved[0]
    recv_off = moved[1].astype(jnp.int32)
    recv_fill = moved[2].astype(jnp.float32)
    incoming = n_label * most
    recv_q = (
        recv_q.reshape(n_label, clus_dev, most, width)
        .transpose(1, 0, 2, 3)
        .reshape(clus_dev, incoming, width)
    )
    recv_off = (
        recv_off.reshape(n_label, clus_dev, most, n_pos)
        .transpose(1, 0, 2, 3)
        .reshape(clus_dev, incoming, n_pos)
    )
    recv_fill = (
        recv_fill.reshape(n_label, clus_dev, most).transpose(1, 0, 2).reshape(clus_dev, incoming)
    )
    weights = label_weight.reshape(clus_dev, cluster_size, width)
    scores = jnp.einsum("cnd,cld->cnl", recv_q, weights, preferred_element_type=jnp.float32)
    labels = jnp.arange(cluster_size, dtype=jnp.int32)
    positive = jnp.any(recv_off[..., None] == labels, axis=-2).astype(jnp.float32)
    signal = ((jax.nn.sigmoid(scores) - positive) * recv_fill[..., None]).astype(jnp.bfloat16)
    signal_split = signal.reshape(clus_dev, n_label, most, cluster_size)
    part_dq = jnp.einsum(
        "csml,cld->scmd", signal_split, weights, preferred_element_type=jnp.float32
    ).astype(jnp.bfloat16)
    part_dw = jnp.einsum("cnl,cnd->cld", signal, recv_q, preferred_element_type=jnp.float32)
    part_dw = part_dw.reshape(clus_dev * cluster_size, width)
    back = lax.all_to_all(
        part_dq.reshape(n_label, rows_dev, width), "label", split_axis=0, concat_axis=0, tiled=True
    )
    back_rows = back.reshape(clusters * most, width)[target]
    query_grad = jnp.sum(back_rows.reshape(q_dev, beam, width).astype(jnp.float32), axis=1)
    summed = lax.psum_scatter(part_dw, "dp", scatter_dimension=0, tiled=True)
    share = summed.shape[0]
    own_rows = lax.dynamic_slice_in_dim(
        label_weight, lax.axis_index("dp") * share, share, 0
    ).astype(jnp.float32)
    return (query_grad, own_rows - STEP_SIZE * summed)


MESH = pl.DeviceIdType.MESH
SLOTS = 16
CHUNK = 8


def tn_dot(a, b):
    return lax.dot_general(a, b, (((0,), (0,)), ((), ())), preferred_element_type=jnp.float32)


def nt_dot(a, b):
    return lax.dot_general(a, b, (((1,), (1,)), ((), ())), preferred_element_type=jnp.float32)


def pick_matrix(meta, beam, first):
    q_dev = meta.shape[1]
    ids = (first + lax.broadcasted_iota(jnp.int32, (CHUNK, q_dev), 0)).astype(jnp.float32)
    member = meta[32:33, :] == ids
    for j in range(1, beam):
        member = member | (meta[32 + j:33 + j, :] == ids)
    member = member.astype(jnp.float32)
    row = lax.broadcasted_iota(jnp.int32, (q_dev, q_dev), 0)
    col = lax.broadcasted_iota(jnp.int32, (q_dev, q_dev), 1)
    upper = (row < col).astype(jnp.float32).astype(jnp.bfloat16)
    rank = jnp.dot(member.astype(jnp.bfloat16), upper, preferred_element_type=jnp.float32)
    code = jnp.where(member > 0, rank, -1.0)
    wide = jnp.broadcast_to(code[:, None, :], (CHUNK, SLOTS, q_dev))
    place = lax.broadcasted_iota(jnp.int32, (CHUNK, SLOTS, q_dev), 1).astype(jnp.float32)
    pick = (wide == place).astype(jnp.float32).reshape(CHUNK * SLOTS, q_dev)
    return pick.astype(jnp.bfloat16)


def gather_chunk(blk_ref, src, b, first, at, beam, x_ref, off_ref):
    q_dev = blk_ref.shape[2]
    tiles = (blk_ref.shape[1] - 64) // q_dev
    meta = blk_ref[src, tiles * q_dev:tiles * q_dev + 64, :]
    pick = pick_matrix(meta.astype(jnp.float32), beam, first)
    q = jnp.concatenate([blk_ref[src, k * q_dev:(k + 1) * q_dev, :] for k in range(tiles)], axis=1)
    rows = jnp.dot(pick, q, preferred_element_type=jnp.float32).astype(jnp.bfloat16)
    here = pl.ds(pl.multiple_of(b * SLOTS, SLOTS), SLOTS)
    x_ref[pl.ds(at, CHUNK), here, :] = rows.reshape(CHUNK, SLOTS, rows.shape[1])
    high = nt_dot(pick, meta[0:16, :])
    low = nt_dot(pick, meta[16:32, :])
    cluster = first + lax.broadcasted_iota(jnp.int32, high.shape, 0) // SLOTS
    off = jnp.where(high == cluster.astype(jnp.float32), low, -1.0)
    off_ref[pl.ds(at, CHUNK), here, :] = off.reshape(CHUNK, SLOTS, 16)
    return pick


def signal_of(x, off, w, n_pos):
    score = nt_dot(x, w)
    label = lax.broadcasted_iota(jnp.int32, score.shape, 1).astype(jnp.float32)
    hit = off[:, 0:1] == label
    for p in range(1, n_pos):
        hit = hit | (off[:, p:p + 1] == label)
    return (jax.nn.sigmoid(score) - hit.astype(jnp.float32)).astype(jnp.bfloat16)


def flip(l, j):
    return ((l // 4 + j // 4) % 2) * 4 + ((l // 2 + j // 2) % 2) * 2 + (l + j) % 2


def step_kernel(n_dp, n_label, beam, n_pos, mine_ref, w_hbm, grad_ref, new_ref,
                blk_ref, w_ref, x_ref, y_ref, pick_ref, off_ref, sig_ref, part_ref, back_ref,
                local_sem, recv_sem, half_sem, z_sem, send_sem, back_send, back_recv):
    d, l = lax.axis_index("dp"), lax.axis_index("label")
    clus_dev = w_ref.shape[0]
    chunks = clus_dev // CHUNK
    rows = CHUNK * SLOTS
    length = blk_ref.shape[1]
    half = length // 2
    xn, yn, sib, diag = flip(l, 2), flip(l, 4), flip(l, 1), flip(l, 6)
    whole, first, second = pl.ds(0, length), pl.ds(0, half), pl.ds(half, half)
    near = jnp.where(d == 0, 1, jnp.where(d == 1, 0, jnp.where(d == 2, 3, 2)))
    mid = jnp.where(d == 0, 2, jnp.where(d == 1, 2, 1))
    far = jnp.where(d < 2, 3, 0)
    planes = [d, near, mid, far]

    load_w = pltpu.make_async_copy(w_hbm, w_ref, local_sem.at[0])
    load_w.start()
    load_q = pltpu.make_async_copy(mine_ref, blk_ref.at[d * n_label + l], local_sem.at[1])
    load_q.start()

    barrier = pltpu.get_barrier_semaphore()
    for j in range(1, n_label):
        pl.semaphore_signal(barrier, inc=1, device_id=(d, flip(l, j)), device_id_type=MESH)
    for p in planes[1:]:
        pl.semaphore_signal(barrier, inc=1, device_id=(p, l), device_id_type=MESH)
    pl.semaphore_wait(barrier, n_label - 1 + n_dp - 1)

    def copy(g, part, send, recv, to):
        return pltpu.make_async_remote_copy(
            src_ref=blk_ref.at[g, part], dst_ref=blk_ref.at[g, part], send_sem=send,
            recv_sem=recv, device_id=to, device_id_type=MESH,
        )

    def z_copy(s):
        g = d * n_label + l
        return copy(g, whole, z_sem.at[s - 1], recv_sem.at[g], (planes[s], l))

    def arrived(g, part, sem):
        copy(g, part, z_sem.at[0], sem, (d, sib)).wait_recv()

    def sends(s):
        base = planes[s] * n_label
        own, gx, gy, gd = base + l, base + xn, base + yn, base + diag
        sem = [send_sem.at[s * 8 + i] for i in range(8)]
        return [
            (own, whole, sem[0], recv_sem.at[own], (d, xn)),
            (own, whole, sem[1], recv_sem.at[own], (d, yn)),
            (own, whole, sem[2], recv_sem.at[own], (d, sib)),
            (gx, first, sem[3], recv_sem.at[gx], (d, yn)),
            (gx, whole, sem[4], recv_sem.at[gx], (d, sib)),
            (gy, second, sem[5], half_sem.at[planes[s]], (d, xn)),
            (gy, whole, sem[6], recv_sem.at[gy], (d, sib)),
            (gd, whole, sem[7], recv_sem.at[gd], (d, sib)),
        ]

    def stage_a(s):
        g = planes[s] * n_label + l
        if s > 0:
            arrived(g, whole, recv_sem.at[g])
        for c in sends(s)[:3]:
            copy(*c).start()

    def stage_b(s):
        gx, gy = planes[s] * n_label + xn, planes[s] * n_label + yn
        arrived(gx, whole, recv_sem.at[gx])
        for c in sends(s)[3:5]:
            copy(*c).start()
        arrived(gy, whole, recv_sem.at[gy])
        for c in sends(s)[5:7]:
            copy(*c).start()

    def stage_c(s):
        g = planes[s] * n_label + diag
        arrived(g, first, recv_sem.at[g])
        arrived(g, second, half_sem.at[planes[s]])
        copy(*sends(s)[7]).start()

    def stage_d(s):
        for j in (1, 3, 5, 7):
            g = planes[s] * n_label + flip(l, j)
            arrived(g, whole, recv_sem.at[g])

    def gather_own(start, stop, stride):
        @pl.loop(0, (stop - start + stride - 1) // stride)
        def _(i):
            j = start + i * stride
            for h in range(chunks):
                pick = gather_chunk(
                    blk_ref, d * n_label + flip(l, j), j, l * clus_dev + h * CHUNK, h * CHUNK,
                    beam, x_ref, off_ref,
                )
                pick_ref[j, h * rows:(h + 1) * rows, :] = pick

    def signals(start, stop):
        @pl.loop(start // 2, stop // 2)
        def _(c2):
            for u in range(2):
                c = c2 * 2 + u
                w = w_ref[c]
                sig = signal_of(x_ref[c], off_ref[c], w, n_pos)
                sig_ref[c] = sig
                y_ref[c] = jnp.dot(sig, w, preferred_element_type=jnp.float32).astype(jnp.bfloat16)

    def grad_copy(j):
        return pltpu.make_async_remote_copy(
            src_ref=part_ref.at[j], dst_ref=back_ref.at[j], send_sem=back_send.at[j],
            recv_sem=back_recv.at[j], device_id=(d, flip(l, j)), device_id_type=MESH,
        )

    def part_of(j):
        y = y_ref[:, j * SLOTS:(j + 1) * SLOTS, :].reshape(clus_dev * SLOTS, y_ref.shape[2])
        return tn_dot(pick_ref[j], y)

    load_q.wait()
    stage_a(0)
    for s in range(1, n_dp):
        z_copy(s).start()
    gather_own(0, 1, 1)
    stage_b(0)
    gather_own(2, 5, 2)
    stage_c(0)
    stage_a(1)
    gather_own(6, 7, 1)
    stage_d(0)
    stage_b(1)
    gather_own(1, 8, 2)
    stage_c(1)
    stage_a(2)
    load_w.wait()
    signals(0, clus_dev // 2)
    stage_b(2)
    stage_a(3)
    signals(clus_dev // 2, clus_dev)
    stage_c(2)
    stage_b(3)
    for j in (7, 6, 5, 3, 4, 2, 1):
        part_ref[j] = part_of(j).astype(jnp.bfloat16)
        grad_copy(j).start()
    stage_c(3)
    grad_ref[...] = part_of(0)

    @pl.loop(0, CHUNK)
    def _(c):
        at = d * CHUNK + c
        new_ref[c] = w_ref[at].astype(jnp.float32) - STEP_SIZE * tn_dot(sig_ref[at], x_ref[at])

    for s in range(1, n_dp):
        stage_d(s)

        @pl.loop(0, n_label // 2)
        def _(i):
            for u in range(2):
                j = i * 2 + u
                gather_chunk(
                    blk_ref, planes[s] * n_label + j, j, l * clus_dev + d * CHUNK, 0, beam,
                    x_ref, off_ref,
                )

        @pl.loop(0, CHUNK // 2)
        def _(c2):
            for u in range(2):
                c = c2 * 2 + u
                x = x_ref[c]
                sig = signal_of(x, off_ref[c], w_ref[d * CHUNK + c], n_pos)
                new_ref[c] = new_ref[c] - STEP_SIZE * tn_dot(sig, x)

    for j in range(1, n_label):
        grad_copy(j).wait_recv()
    total = grad_ref[...]
    for j in range(1, n_label):
        total = total + back_ref[j].astype(jnp.float32)
    grad_ref[...] = total
    for j in range(1, n_label):
        grad_copy(j).wait_send()
    for s in range(1, n_dp):
        z_copy(s).wait_send()
    for s in range(n_dp):
        for c in sends(s):
            copy(*c).wait_send()


def make_block(queries, beams, positive_slots, owner, cluster_size):
    q_dev, width = queries.shape
    beam, n_pos = beams.shape[1], positive_slots.shape[1]
    ids = jnp.arange(owner.shape[0], dtype=jnp.int32)
    lookup = beams[:, :, None] == ids[None, None, :]
    slot = jnp.sum(jnp.where(lookup, owner[None, None, :], 0), axis=2)
    where_p = positive_slots[:, :, None] // cluster_size == jnp.arange(beam, dtype=jnp.int32)
    pos_slot = jnp.sum(jnp.where(where_p, slot[:, None, :], 0), axis=2)
    pos_label = positive_slots % cluster_size
    meta = jnp.concatenate(
        [
            jnp.pad(pos_slot, ((0, 0), (0, 16 - n_pos))),
            jnp.pad(pos_label, ((0, 0), (0, 16 - n_pos))),
            jnp.pad(slot, ((0, 0), (0, 32 - beam)), constant_values=-1),
        ],
        axis=1,
    )
    tiles = queries.reshape(q_dev, width // q_dev, q_dev).transpose(1, 0, 2).reshape(width, q_dev)
    return jnp.concatenate([tiles, meta.T.astype(jnp.bfloat16)], axis=0)


def sparse_body(queries, beams, positive_slots, owner, label_weight):
    n_label = lax.axis_size("label")
    n_dp = lax.axis_size("dp")
    q_dev, width = queries.shape
    clus_dev = owner.shape[0] // n_label
    cluster_size = label_weight.shape[0] // clus_dev
    block = make_block(queries, beams, positive_slots, owner, cluster_size)
    slots = n_label * SLOTS
    length = block.shape[0]
    grad, new = pl.pallas_call(
        functools.partial(step_kernel, n_dp, n_label, beams.shape[1], positive_slots.shape[1]),
        out_shape=(
            jax.ShapeDtypeStruct((q_dev, width), jnp.float32),
            jax.ShapeDtypeStruct((CHUNK, cluster_size, width), jnp.float32),
        ),
        in_specs=[pl.BlockSpec(memory_space=pl.ANY)] * 2,
        out_specs=(pl.BlockSpec(memory_space=pltpu.VMEM),) * 2,
        scratch_shapes=[
            pltpu.VMEM((n_dp * n_label, length, q_dev), jnp.bfloat16),
            pltpu.VMEM((clus_dev, cluster_size, width), jnp.bfloat16),
            pltpu.VMEM((clus_dev, slots, width), jnp.bfloat16),
            pltpu.VMEM((clus_dev, slots, width), jnp.bfloat16),
            pltpu.VMEM((n_label, clus_dev * SLOTS, q_dev), jnp.bfloat16),
            pltpu.VMEM((clus_dev, slots, 16), jnp.float32),
            pltpu.VMEM((clus_dev, slots, cluster_size), jnp.bfloat16),
            pltpu.VMEM((n_label, q_dev, width), jnp.bfloat16),
            pltpu.VMEM((n_label, q_dev, width), jnp.bfloat16),
            pltpu.SemaphoreType.DMA((2,)),
            pltpu.SemaphoreType.DMA((n_dp * n_label,)),
            pltpu.SemaphoreType.DMA((n_dp,)),
            pltpu.SemaphoreType.DMA((n_dp - 1,)),
            pltpu.SemaphoreType.DMA((8 * n_dp,)),
            pltpu.SemaphoreType.DMA((n_label,)),
            pltpu.SemaphoreType.DMA((n_label,)),
        ],
        compiler_params=pltpu.CompilerParams(
            vmem_limit_bytes=58 << 20, collective_id=0, has_side_effects=True
        ),
    )(block, label_weight.reshape(clus_dev, cluster_size, width))
    return (grad, new.reshape(CHUNK * cluster_size, width))


def choose(queries, beams, positive_slots, owner, label_weight):
    n_dp, n_label = lax.axis_size("dp"), lax.axis_size("label")
    q_dev, width = queries.shape
    fits = n_dp == 4 and n_label == 8 and queries.size * n_dp * n_label * 2 <= (8 << 20) and n_label * SLOTS == q_dev
    fits = fits and q_dev == 128 and width % q_dev == 0 and beams.shape[1] <= 32
    fits = fits and owner.shape[0] == n_label * n_dp * CHUNK and positive_slots.shape[1] <= 16
    fits = fits and max(2, q_dev * 3 // 32) <= SLOTS and owner.shape[0] <= 256
    form = sparse_body if fits else body
    return form(queries, beams, positive_slots, owner, label_weight)


def solution(mesh):
    in_specs = (
        P(("dp", "label"), None),
        P(("dp", "label"), None),
        P(("dp", "label"), None),
        P(),
        P("label", None),
    )
    out_specs = (P(("dp", "label"), None), P(("label", "dp"), None))
    return jax.shard_map(
        choose, mesh=mesh, in_specs=in_specs, out_specs=out_specs, check_vma=False
    )
```

```python
import functools

import jax
import jax.numpy as jnp
from jax import lax
from jax.experimental import pallas as pl
from jax.experimental.pallas import tpu as pltpu
from jax.sharding import PartitionSpec as P

STEP_SIZE = 0.02


def slot_table(keys, count, most):
    q_rows, beam = keys.shape
    pairs = q_rows * beam
    ids = jnp.arange(count, dtype=jnp.int32)
    member = jnp.any(keys[:, :, None] == ids[None, None, :], axis=1).astype(jnp.float32)
    row_ids = jnp.arange(q_rows, dtype=jnp.int32)
    lower = (row_ids[:, None] > row_ids[None, :]).astype(jnp.float32)
    before = jnp.dot(lower, member, precision=lax.Precision.HIGHEST)
    safe_keys = jnp.minimum(keys, count - 1)
    rank = jnp.take_along_axis(before, safe_keys, axis=1).astype(jnp.int32)
    flat_keys = keys.reshape(pairs)
    target = jnp.where(flat_keys < count, flat_keys * most + rank.reshape(pairs), count * most)
    table = (
        jnp.full((count * most,), pairs, jnp.int32)
        .at[target]
        .set(jnp.arange(pairs, dtype=jnp.int32), mode="drop")
    )
    return (target, table)


def body(queries, beams, positive_slots, owner, label_weight):
    n_label = lax.axis_size("label")
    q_dev, width = queries.shape
    beam = beams.shape[1]
    n_pos = positive_slots.shape[1]
    clusters = owner.shape[0]
    clus_dev = clusters // n_label
    cluster_size = label_weight.shape[0] // clus_dev
    most = max(2, q_dev * 3 // 32)
    pairs = q_dev * beam
    rows_dev = clus_dev * most
    lookup = beams[:, :, None] == jnp.arange(clusters, dtype=jnp.int32)[None, None, :]
    pair_slot = jnp.sum(jnp.where(lookup, owner[None, None, :], 0), axis=2)
    position = jnp.arange(beam, dtype=jnp.int32)
    inside = positive_slots[:, None, :] // cluster_size == position[None, :, None]
    pair_offset = jnp.where(inside, positive_slots[:, None, :] % cluster_size, -1)
    target, table = slot_table(pair_slot, clusters, most)
    filled = table < pairs
    padded = jnp.concatenate([queries, jnp.zeros((1, width), queries.dtype)], axis=0)
    send_q = padded[jnp.where(filled, table // beam, q_dev)]
    flat_off = pair_offset.reshape(pairs, n_pos)
    send_off = jnp.where(filled[:, None], flat_off[jnp.where(filled, table, 0)], -1)
    moved = (
        lax.all_to_all(
            send_q.reshape(n_label, rows_dev, width),
            "label",
            split_axis=0,
            concat_axis=0,
            tiled=True,
        ),
        lax.all_to_all(
            send_off.astype(jnp.bfloat16).reshape(n_label, rows_dev, n_pos),
            "label",
            split_axis=0,
            concat_axis=0,
            tiled=True,
        ),
        lax.all_to_all(
            filled.astype(jnp.bfloat16).reshape(n_label, rows_dev),
            "label",
            split_axis=0,
            concat_axis=0,
            tiled=True,
        ),
    )
    recv_q = moved[0]
    recv_off = moved[1].astype(jnp.int32)
    recv_fill = moved[2].astype(jnp.float32)
    incoming = n_label * most
    recv_q = (
        recv_q.reshape(n_label, clus_dev, most, width)
        .transpose(1, 0, 2, 3)
        .reshape(clus_dev, incoming, width)
    )
    recv_off = (
        recv_off.reshape(n_label, clus_dev, most, n_pos)
        .transpose(1, 0, 2, 3)
        .reshape(clus_dev, incoming, n_pos)
    )
    recv_fill = (
        recv_fill.reshape(n_label, clus_dev, most).transpose(1, 0, 2).reshape(clus_dev, incoming)
    )
    weights = label_weight.reshape(clus_dev, cluster_size, width)
    scores = jnp.einsum("cnd,cld->cnl", recv_q, weights, preferred_element_type=jnp.float32)
    labels = jnp.arange(cluster_size, dtype=jnp.int32)
    positive = jnp.any(recv_off[..., None] == labels, axis=-2).astype(jnp.float32)
    signal = ((jax.nn.sigmoid(scores) - positive) * recv_fill[..., None]).astype(jnp.bfloat16)
    signal_split = signal.reshape(clus_dev, n_label, most, cluster_size)
    part_dq = jnp.einsum(
        "csml,cld->scmd", signal_split, weights, preferred_element_type=jnp.float32
    ).astype(jnp.bfloat16)
    part_dw = jnp.einsum("cnl,cnd->cld", signal, recv_q, preferred_element_type=jnp.float32)
    part_dw = part_dw.reshape(clus_dev * cluster_size, width)
    back = lax.all_to_all(
        part_dq.reshape(n_label, rows_dev, width), "label", split_axis=0, concat_axis=0, tiled=True
    )
    back_rows = back.reshape(clusters * most, width)[target]
    query_grad = jnp.sum(back_rows.reshape(q_dev, beam, width).astype(jnp.float32), axis=1)
    summed = lax.psum_scatter(part_dw, "dp", scatter_dimension=0, tiled=True)
    share = summed.shape[0]
    own_rows = lax.dynamic_slice_in_dim(
        label_weight, lax.axis_index("dp") * share, share, 0
    ).astype(jnp.float32)
    return (query_grad, own_rows - STEP_SIZE * summed)


MESH = pl.DeviceIdType.MESH
SLOTS = 16
CHUNK = 8


def tn_dot(a, b):
    return lax.dot_general(a, b, (((0,), (0,)), ((), ())), preferred_element_type=jnp.float32)


def nt_dot(a, b):
    return lax.dot_general(a, b, (((1,), (1,)), ((), ())), preferred_element_type=jnp.float32)


def pick_matrix(meta, beam, first):
    q_dev = meta.shape[1]
    ids = (first + lax.broadcasted_iota(jnp.int32, (CHUNK, q_dev), 0)).astype(jnp.float32)
    member = meta[32:33, :] == ids
    for j in range(1, beam):
        member = member | (meta[32 + j:33 + j, :] == ids)
    member = member.astype(jnp.float32)
    row = lax.broadcasted_iota(jnp.int32, (q_dev, q_dev), 0)
    col = lax.broadcasted_iota(jnp.int32, (q_dev, q_dev), 1)
    upper = (row < col).astype(jnp.float32).astype(jnp.bfloat16)
    rank = jnp.dot(member.astype(jnp.bfloat16), upper, preferred_element_type=jnp.float32)
    code = jnp.where(member > 0, rank, -1.0)
    wide = jnp.broadcast_to(code[:, None, :], (CHUNK, SLOTS, q_dev))
    place = lax.broadcasted_iota(jnp.int32, (CHUNK, SLOTS, q_dev), 1).astype(jnp.float32)
    pick = (wide == place).astype(jnp.float32).reshape(CHUNK * SLOTS, q_dev)
    return pick.astype(jnp.bfloat16)


def gather_chunk(blk_ref, src, b, first, at, beam, x_ref, off_ref):
    q_dev = blk_ref.shape[2]
    tiles = (blk_ref.shape[1] - 64) // q_dev
    meta = blk_ref[src, tiles * q_dev:tiles * q_dev + 64, :]
    pick = pick_matrix(meta.astype(jnp.float32), beam, first)
    q = jnp.concatenate([blk_ref[src, k * q_dev:(k + 1) * q_dev, :] for k in range(tiles)], axis=1)
    rows = jnp.dot(pick, q, preferred_element_type=jnp.float32).astype(jnp.bfloat16)
    here = pl.ds(pl.multiple_of(b * SLOTS, SLOTS), SLOTS)
    x_ref[pl.ds(at, CHUNK), here, :] = rows.reshape(CHUNK, SLOTS, rows.shape[1])
    high = nt_dot(pick, meta[0:16, :])
    low = nt_dot(pick, meta[16:32, :])
    cluster = first + lax.broadcasted_iota(jnp.int32, high.shape, 0) // SLOTS
    off = jnp.where(high == cluster.astype(jnp.float32), low, -1.0)
    off_ref[pl.ds(at, CHUNK), here, :] = off.reshape(CHUNK, SLOTS, 16)
    return pick


def signal_of(x, off, w, n_pos):
    score = nt_dot(x, w)
    label = lax.broadcasted_iota(jnp.int32, score.shape, 1).astype(jnp.float32)
    hit = off[:, 0:1] == label
    for p in range(1, n_pos):
        hit = hit | (off[:, p:p + 1] == label)
    return (jax.nn.sigmoid(score) - hit.astype(jnp.float32)).astype(jnp.bfloat16)


def flip(l, j):
    return ((l // 4 + j // 4) % 2) * 4 + ((l // 2 + j // 2) % 2) * 2 + (l + j) % 2


def step_kernel(n_dp, n_label, beam, n_pos, mine_ref, w_hbm, grad_ref, new_ref,
                blk_ref, w_ref, x_ref, y_ref, pick_ref, off_ref, sig_ref, part_ref, back_ref,
                local_sem, recv_sem, half_sem, z_sem, send_sem, back_send, back_recv):
    d, l = lax.axis_index("dp"), lax.axis_index("label")
    clus_dev = w_ref.shape[0]
    chunks = clus_dev // CHUNK
    rows = CHUNK * SLOTS
    length = blk_ref.shape[1]
    half = length // 2
    xn, yn, sib, diag = flip(l, 2), flip(l, 4), flip(l, 1), flip(l, 6)
    whole, first, second = pl.ds(0, length), pl.ds(0, half), pl.ds(half, half)
    near = jnp.where(d == 0, 1, jnp.where(d == 1, 0, jnp.where(d == 2, 3, 2)))
    mid = jnp.where(d == 0, 2, jnp.where(d == 1, 2, 1))
    far = jnp.where(d < 2, 3, 0)
    planes = [d, near, mid, far]
    inner = (d == 1) | (d == 2)
    toward = jnp.where(d < 2, d + 1, d - 1)
    outward = jnp.where(d == 1, 0, 3)

    load_w = pltpu.make_async_copy(w_hbm, w_ref, local_sem.at[0])
    load_w.start()
    load_q = pltpu.make_async_copy(mine_ref, blk_ref.at[d * n_label + l], local_sem.at[1])
    load_q.start()

    barrier = pltpu.get_barrier_semaphore()
    for j in range(1, n_label):
        pl.semaphore_signal(barrier, inc=1, device_id=(d, flip(l, j)), device_id_type=MESH)
    for p in planes[1:]:
        pl.semaphore_signal(barrier, inc=1, device_id=(p, l), device_id_type=MESH)
    pl.semaphore_wait(barrier, n_label - 1 + n_dp - 1)

    def copy(g, part, send, recv, to):
        return pltpu.make_async_remote_copy(
            src_ref=blk_ref.at[g, part], dst_ref=blk_ref.at[g, part], send_sem=send,
            recv_sem=recv, device_id=to, device_id_type=MESH,
        )

    def z_copy(s):
        g = planes[s] * n_label + l
        onward = jnp.where(planes[s] < d, d + 1, d - 1)
        to = outward if s == 0 else jnp.minimum(onward, n_dp - 1)
        return copy(g, whole, z_sem.at[s], recv_sem.at[g], (to, l))

    def z_first():
        g = d * n_label + l
        return copy(g, whole, z_sem.at[n_dp], recv_sem.at[g], (toward, l))

    def arrived(g, part, sem):
        copy(g, part, z_sem.at[0], sem, (d, sib)).wait_recv()

    def sends(s):
        base = planes[s] * n_label
        own, gx, gy, gd = base + l, base + xn, base + yn, base + diag
        sem = [send_sem.at[s * 8 + i] for i in range(8)]
        return [
            (own, whole, sem[0], recv_sem.at[own], (d, xn)),
            (own, whole, sem[1], recv_sem.at[own], (d, yn)),
            (own, whole, sem[2], recv_sem.at[own], (d, sib)),
            (gx, first, sem[3], recv_sem.at[gx], (d, yn)),
            (gx, whole, sem[4], recv_sem.at[gx], (d, sib)),
            (gy, second, sem[5], half_sem.at[planes[s]], (d, xn)),
            (gy, whole, sem[6], recv_sem.at[gy], (d, sib)),
            (gd, whole, sem[7], recv_sem.at[gd], (d, sib)),
        ]

    def stage_a(s):
        g = planes[s] * n_label + l
        if s > 0:
            arrived(g, whole, recv_sem.at[g])
        else:
            z_first().start()

        @pl.when(inner)
        def _():
            z_copy(s).start()

        for c in sends(s)[:3]:
            copy(*c).start()

    def stage_b(s):
        gx, gy = planes[s] * n_label + xn, planes[s] * n_label + yn
        arrived(gx, whole, recv_sem.at[gx])
        for c in sends(s)[3:5]:
            copy(*c).start()
        arrived(gy, whole, recv_sem.at[gy])
        for c in sends(s)[5:7]:
            copy(*c).start()

    def stage_c(s):
        g = planes[s] * n_label + diag
        arrived(g, first, recv_sem.at[g])
        arrived(g, second, half_sem.at[planes[s]])
        copy(*sends(s)[7]).start()

    def stage_d(s):
        for j in (1, 3, 5, 7):
            g = planes[s] * n_label + flip(l, j)
            arrived(g, whole, recv_sem.at[g])

    def gather_own(start, stop, stride):
        @pl.loop(0, (stop - start + stride - 1) // stride)
        def _(i):
            j = start + i * stride
            for h in range(chunks):
                pick = gather_chunk(
                    blk_ref, d * n_label + flip(l, j), j, l * clus_dev + h * CHUNK, h * CHUNK,
                    beam, x_ref, off_ref,
                )
                pick_ref[j, h * rows:(h + 1) * rows, :] = pick

    def signals(start, stop):
        @pl.loop(start // 2, stop // 2)
        def _(c2):
            for u in range(2):
                c = c2 * 2 + u
                w = w_ref[c]
                sig = signal_of(x_ref[c], off_ref[c], w, n_pos)
                sig_ref[c] = sig
                y_ref[c] = jnp.dot(sig, w, preferred_element_type=jnp.float32).astype(jnp.bfloat16)

    def grad_copy(j):
        slot = (j - 1) // 2 if j % 2 else 4 + j // 2
        to = sib if j % 2 else flip(l, j)
        return pltpu.make_async_remote_copy(
            src_ref=part_ref.at[j], dst_ref=back_ref.at[slot], send_sem=back_send.at[j],
            recv_sem=back_recv.at[slot], device_id=(d, to), device_id_type=MESH,
        )

    def part_of(j):
        y = y_ref[:, j * SLOTS:(j + 1) * SLOTS, :].reshape(clus_dev * SLOTS, y_ref.shape[2])
        return tn_dot(pick_ref[j], y)

    quarter = clus_dev // 4
    load_q.wait()
    stage_a(0)
    gather_own(0, 1, 1)
    stage_b(0)
    stage_a(1)
    gather_own(2, 5, 2)
    stage_c(0)
    stage_a(2)
    gather_own(6, 7, 1)
    stage_d(0)
    stage_b(1)
    gather_own(1, 4, 2)
    stage_a(3)
    stage_c(1)
    gather_own(5, 8, 2)
    stage_b(2)
    load_w.wait()
    signals(0, quarter)
    stage_c(2)
    stage_b(3)
    signals(quarter, 2 * quarter)
    stage_c(3)
    signals(2 * quarter, clus_dev)
    for j in (7, 3, 5, 1):
        part_ref[j] = part_of(j).astype(jnp.bfloat16)
        grad_copy(j).start()
    for j in (6, 2, 4, 0):
        value = part_of(j)
        grad_copy(j + 1).wait_recv()
        value = value + back_ref[j // 2].astype(jnp.float32)
        if j:
            part_ref[j] = value.astype(jnp.bfloat16)
            grad_copy(j).start()
        else:
            grad_ref[...] = value

    @pl.loop(0, CHUNK)
    def _(c):
        at = d * CHUNK + c
        new_ref[c] = w_ref[at].astype(jnp.float32) - STEP_SIZE * tn_dot(sig_ref[at], x_ref[at])

    for s in range(1, n_dp):
        stage_d(s)

        @pl.loop(0, n_label // 2)
        def _(i):
            for u in range(2):
                j = i * 2 + u
                gather_chunk(
                    blk_ref, planes[s] * n_label + j, j, l * clus_dev + d * CHUNK, 0, beam,
                    x_ref, off_ref,
                )

        @pl.loop(0, CHUNK // 2)
        def _(c2):
            for u in range(2):
                c = c2 * 2 + u
                x = x_ref[c]
                sig = signal_of(x, off_ref[c], w_ref[d * CHUNK + c], n_pos)
                new_ref[c] = new_ref[c] - STEP_SIZE * tn_dot(sig, x)

    total = grad_ref[...]
    for j in (2, 4, 6):
        grad_copy(j).wait_recv()
        total = total + back_ref[4 + j // 2].astype(jnp.float32)
    grad_ref[...] = total
    for j in range(1, n_label):
        grad_copy(j).wait_send()
    z_first().wait_send()

    @pl.when(inner)
    def _():
        for s in range(n_dp):
            z_copy(s).wait_send()

    for s in range(n_dp):
        for c in sends(s):
            copy(*c).wait_send()


def make_block(queries, beams, positive_slots, owner, cluster_size):
    q_dev, width = queries.shape
    beam, n_pos = beams.shape[1], positive_slots.shape[1]
    ids = jnp.arange(owner.shape[0], dtype=jnp.int32)
    lookup = beams[:, :, None] == ids[None, None, :]
    slot = jnp.sum(jnp.where(lookup, owner[None, None, :], 0), axis=2)
    where_p = positive_slots[:, :, None] // cluster_size == jnp.arange(beam, dtype=jnp.int32)
    pos_slot = jnp.sum(jnp.where(where_p, slot[:, None, :], 0), axis=2)
    pos_label = positive_slots % cluster_size
    meta = jnp.concatenate(
        [
            jnp.pad(pos_slot, ((0, 0), (0, 16 - n_pos))),
            jnp.pad(pos_label, ((0, 0), (0, 16 - n_pos))),
            jnp.pad(slot, ((0, 0), (0, 32 - beam)), constant_values=-1),
        ],
        axis=1,
    )
    tiles = queries.reshape(q_dev, width // q_dev, q_dev).transpose(1, 0, 2).reshape(width, q_dev)
    return jnp.concatenate([tiles, meta.T.astype(jnp.bfloat16)], axis=0)


def sparse_body(queries, beams, positive_slots, owner, label_weight):
    n_label = lax.axis_size("label")
    n_dp = lax.axis_size("dp")
    q_dev, width = queries.shape
    clus_dev = owner.shape[0] // n_label
    cluster_size = label_weight.shape[0] // clus_dev
    block = make_block(queries, beams, positive_slots, owner, cluster_size)
    slots = n_label * SLOTS
    length = block.shape[0]
    grad, new = pl.pallas_call(
        functools.partial(step_kernel, n_dp, n_label, beams.shape[1], positive_slots.shape[1]),
        out_shape=(
            jax.ShapeDtypeStruct((q_dev, width), jnp.float32),
            jax.ShapeDtypeStruct((CHUNK, cluster_size, width), jnp.float32),
        ),
        in_specs=[pl.BlockSpec(memory_space=pl.ANY)] * 2,
        out_specs=(pl.BlockSpec(memory_space=pltpu.VMEM),) * 2,
        scratch_shapes=[
            pltpu.VMEM((n_dp * n_label, length, q_dev), jnp.bfloat16),
            pltpu.VMEM((clus_dev, cluster_size, width), jnp.bfloat16),
            pltpu.VMEM((clus_dev, slots, width), jnp.bfloat16),
            pltpu.VMEM((clus_dev, slots, width), jnp.bfloat16),
            pltpu.VMEM((n_label, clus_dev * SLOTS, q_dev), jnp.bfloat16),
            pltpu.VMEM((clus_dev, slots, 16), jnp.float32),
            pltpu.VMEM((clus_dev, slots, cluster_size), jnp.bfloat16),
            pltpu.VMEM((n_label, q_dev, width), jnp.bfloat16),
            pltpu.VMEM((n_label, q_dev, width), jnp.bfloat16),
            pltpu.SemaphoreType.DMA((2,)),
            pltpu.SemaphoreType.DMA((n_dp * n_label,)),
            pltpu.SemaphoreType.DMA((n_dp,)),
            pltpu.SemaphoreType.DMA((n_dp + 1,)),
            pltpu.SemaphoreType.DMA((8 * n_dp,)),
            pltpu.SemaphoreType.DMA((n_label,)),
            pltpu.SemaphoreType.DMA((n_label,)),
        ],
        compiler_params=pltpu.CompilerParams(
            vmem_limit_bytes=58 << 20, collective_id=0, has_side_effects=True
        ),
    )(block, label_weight.reshape(clus_dev, cluster_size, width))
    return (grad, new.reshape(CHUNK * cluster_size, width))


def choose(queries, beams, positive_slots, owner, label_weight):
    n_dp, n_label = lax.axis_size("dp"), lax.axis_size("label")
    q_dev, width = queries.shape
    fits = n_dp == 4 and n_label == 8 and queries.size * n_dp * n_label * 2 <= (8 << 20) and n_label * SLOTS == q_dev
    fits = fits and q_dev == 128 and width % q_dev == 0 and beams.shape[1] <= 32
    fits = fits and owner.shape[0] == n_label * n_dp * CHUNK and positive_slots.shape[1] <= 16
    fits = fits and max(2, q_dev * 3 // 32) <= SLOTS and owner.shape[0] <= 256
    form = sparse_body if fits else body
    return form(queries, beams, positive_slots, owner, label_weight)


def solution(mesh):
    in_specs = (
        P(("dp", "label"), None),
        P(("dp", "label"), None),
        P(("dp", "label"), None),
        P(),
        P("label", None),
    )
    out_specs = (P(("dp", "label"), None), P(("label", "dp"), None))
    return jax.shard_map(
        choose, mesh=mesh, in_specs=in_specs, out_specs=out_specs, check_vma=False
    )
```

```python
import functools

import jax
import jax.numpy as jnp
from jax import lax
from jax.experimental import pallas as pl
from jax.experimental.pallas import tpu as pltpu
from jax.sharding import PartitionSpec as P

STEP_SIZE = 0.02


def slot_table(keys, count, most):
    q_rows, beam = keys.shape
    pairs = q_rows * beam
    ids = jnp.arange(count, dtype=jnp.int32)
    member = jnp.any(keys[:, :, None] == ids[None, None, :], axis=1).astype(jnp.float32)
    row_ids = jnp.arange(q_rows, dtype=jnp.int32)
    lower = (row_ids[:, None] > row_ids[None, :]).astype(jnp.float32)
    before = jnp.dot(lower, member, precision=lax.Precision.HIGHEST)
    safe_keys = jnp.minimum(keys, count - 1)
    rank = jnp.take_along_axis(before, safe_keys, axis=1).astype(jnp.int32)
    flat_keys = keys.reshape(pairs)
    target = jnp.where(flat_keys < count, flat_keys * most + rank.reshape(pairs), count * most)
    table = (
        jnp.full((count * most,), pairs, jnp.int32)
        .at[target]
        .set(jnp.arange(pairs, dtype=jnp.int32), mode="drop")
    )
    return (target, table)


def body(queries, beams, positive_slots, owner, label_weight):
    n_label = lax.axis_size("label")
    q_dev, width = queries.shape
    beam = beams.shape[1]
    n_pos = positive_slots.shape[1]
    clusters = owner.shape[0]
    clus_dev = clusters // n_label
    cluster_size = label_weight.shape[0] // clus_dev
    most = max(2, q_dev * 3 // 32)
    pairs = q_dev * beam
    rows_dev = clus_dev * most
    lookup = beams[:, :, None] == jnp.arange(clusters, dtype=jnp.int32)[None, None, :]
    pair_slot = jnp.sum(jnp.where(lookup, owner[None, None, :], 0), axis=2)
    position = jnp.arange(beam, dtype=jnp.int32)
    inside = positive_slots[:, None, :] // cluster_size == position[None, :, None]
    pair_offset = jnp.where(inside, positive_slots[:, None, :] % cluster_size, -1)
    target, table = slot_table(pair_slot, clusters, most)
    filled = table < pairs
    padded = jnp.concatenate([queries, jnp.zeros((1, width), queries.dtype)], axis=0)
    send_q = padded[jnp.where(filled, table // beam, q_dev)]
    flat_off = pair_offset.reshape(pairs, n_pos)
    send_off = jnp.where(filled[:, None], flat_off[jnp.where(filled, table, 0)], -1)
    moved = (
        lax.all_to_all(
            send_q.reshape(n_label, rows_dev, width),
            "label",
            split_axis=0,
            concat_axis=0,
            tiled=True,
        ),
        lax.all_to_all(
            send_off.astype(jnp.bfloat16).reshape(n_label, rows_dev, n_pos),
            "label",
            split_axis=0,
            concat_axis=0,
            tiled=True,
        ),
        lax.all_to_all(
            filled.astype(jnp.bfloat16).reshape(n_label, rows_dev),
            "label",
            split_axis=0,
            concat_axis=0,
            tiled=True,
        ),
    )
    recv_q = moved[0]
    recv_off = moved[1].astype(jnp.int32)
    recv_fill = moved[2].astype(jnp.float32)
    incoming = n_label * most
    recv_q = (
        recv_q.reshape(n_label, clus_dev, most, width)
        .transpose(1, 0, 2, 3)
        .reshape(clus_dev, incoming, width)
    )
    recv_off = (
        recv_off.reshape(n_label, clus_dev, most, n_pos)
        .transpose(1, 0, 2, 3)
        .reshape(clus_dev, incoming, n_pos)
    )
    recv_fill = (
        recv_fill.reshape(n_label, clus_dev, most).transpose(1, 0, 2).reshape(clus_dev, incoming)
    )
    weights = label_weight.reshape(clus_dev, cluster_size, width)
    scores = jnp.einsum("cnd,cld->cnl", recv_q, weights, preferred_element_type=jnp.float32)
    labels = jnp.arange(cluster_size, dtype=jnp.int32)
    positive = jnp.any(recv_off[..., None] == labels, axis=-2).astype(jnp.float32)
    signal = ((jax.nn.sigmoid(scores) - positive) * recv_fill[..., None]).astype(jnp.bfloat16)
    signal_split = signal.reshape(clus_dev, n_label, most, cluster_size)
    part_dq = jnp.einsum(
        "csml,cld->scmd", signal_split, weights, preferred_element_type=jnp.float32
    ).astype(jnp.bfloat16)
    part_dw = jnp.einsum("cnl,cnd->cld", signal, recv_q, preferred_element_type=jnp.float32)
    part_dw = part_dw.reshape(clus_dev * cluster_size, width)
    back = lax.all_to_all(
        part_dq.reshape(n_label, rows_dev, width), "label", split_axis=0, concat_axis=0, tiled=True
    )
    back_rows = back.reshape(clusters * most, width)[target]
    query_grad = jnp.sum(back_rows.reshape(q_dev, beam, width).astype(jnp.float32), axis=1)
    summed = lax.psum_scatter(part_dw, "dp", scatter_dimension=0, tiled=True)
    share = summed.shape[0]
    own_rows = lax.dynamic_slice_in_dim(
        label_weight, lax.axis_index("dp") * share, share, 0
    ).astype(jnp.float32)
    return (query_grad, own_rows - STEP_SIZE * summed)


MESH = pl.DeviceIdType.MESH
SLOTS = 16
CHUNK = 8


def tn_dot(a, b):
    return lax.dot_general(a, b, (((0,), (0,)), ((), ())), preferred_element_type=jnp.float32)


def nt_dot(a, b):
    return lax.dot_general(a, b, (((1,), (1,)), ((), ())), preferred_element_type=jnp.float32)


def pick_matrix(meta, beam, first):
    q_dev = meta.shape[1]
    ids = (first + lax.broadcasted_iota(jnp.int32, (CHUNK, q_dev), 0)).astype(jnp.float32)
    member = meta[32:33, :] == ids
    for j in range(1, beam):
        member = member | (meta[32 + j:33 + j, :] == ids)
    member = member.astype(jnp.float32)
    row = lax.broadcasted_iota(jnp.int32, (q_dev, q_dev), 0)
    col = lax.broadcasted_iota(jnp.int32, (q_dev, q_dev), 1)
    upper = (row < col).astype(jnp.float32).astype(jnp.bfloat16)
    rank = jnp.dot(member.astype(jnp.bfloat16), upper, preferred_element_type=jnp.float32)
    code = jnp.where(member > 0, rank, -1.0)
    wide = jnp.broadcast_to(code[:, None, :], (CHUNK, SLOTS, q_dev))
    place = lax.broadcasted_iota(jnp.int32, (CHUNK, SLOTS, q_dev), 1).astype(jnp.float32)
    pick = (wide == place).astype(jnp.float32).reshape(CHUNK * SLOTS, q_dev)
    return pick.astype(jnp.bfloat16)


def gather_chunk(blk_ref, src, b, first, at, beam, x_ref, off_ref):
    q_dev = blk_ref.shape[2]
    tiles = (blk_ref.shape[1] - 64) // q_dev
    meta = blk_ref[src, tiles * q_dev:tiles * q_dev + 64, :]
    pick = pick_matrix(meta.astype(jnp.float32), beam, first)
    q = jnp.concatenate([blk_ref[src, k * q_dev:(k + 1) * q_dev, :] for k in range(tiles)], axis=1)
    rows = jnp.dot(pick, q, preferred_element_type=jnp.float32).astype(jnp.bfloat16)
    here = pl.ds(pl.multiple_of(b * SLOTS, SLOTS), SLOTS)
    x_ref[pl.ds(at, CHUNK), here, :] = rows.reshape(CHUNK, SLOTS, rows.shape[1])
    high = nt_dot(pick, meta[0:16, :])
    low = nt_dot(pick, meta[16:32, :])
    cluster = first + lax.broadcasted_iota(jnp.int32, high.shape, 0) // SLOTS
    off = jnp.where(high == cluster.astype(jnp.float32), low, -1.0)
    off_ref[pl.ds(at, CHUNK), here, :] = off.reshape(CHUNK, SLOTS, 16)
    return pick


def signal_of(x, off, w, n_pos):
    score = nt_dot(x, w)
    label = lax.broadcasted_iota(jnp.int32, score.shape, 1).astype(jnp.float32)
    hit = off[:, 0:1] == label
    for p in range(1, n_pos):
        hit = hit | (off[:, p:p + 1] == label)
    return (jax.nn.sigmoid(score) - hit.astype(jnp.float32)).astype(jnp.bfloat16)


def flip(l, j):
    return ((l // 4 + j // 4) % 2) * 4 + ((l // 2 + j // 2) % 2) * 2 + (l + j) % 2


def step_kernel(n_dp, n_label, beam, n_pos, mine_ref, w_hbm, grad_ref, new_ref,
                blk_ref, w_ref, x_ref, y_ref, pick_ref, off_ref, sig_ref, part_ref, back_ref,
                local_sem, recv_sem, half_sem, z_sem, send_sem, back_send, back_recv):
    d, l = lax.axis_index("dp"), lax.axis_index("label")
    clus_dev = w_ref.shape[0]
    chunks = clus_dev // CHUNK
    rows = CHUNK * SLOTS
    length = blk_ref.shape[1]
    half = length // 2
    xn, yn, sib, diag = flip(l, 2), flip(l, 4), flip(l, 1), flip(l, 6)
    whole, first, second = pl.ds(0, length), pl.ds(0, half), pl.ds(half, half)
    near = jnp.where(d == 0, 1, jnp.where(d == 1, 0, jnp.where(d == 2, 3, 2)))
    mid = jnp.where(d == 0, 2, jnp.where(d == 1, 2, 1))
    far = jnp.where(d < 2, 3, 0)
    planes = [d, near, mid, far]
    inner = (d == 1) | (d == 2)
    toward = jnp.where(d < 2, d + 1, d - 1)
    outward = jnp.where(d == 1, 0, 3)

    load_w = pltpu.make_async_copy(w_hbm, w_ref, local_sem.at[0])
    load_w.start()
    load_q = pltpu.make_async_copy(mine_ref, blk_ref.at[d * n_label + l], local_sem.at[1])
    load_q.start()

    barrier = pltpu.get_barrier_semaphore()
    for j in range(1, n_label):
        pl.semaphore_signal(barrier, inc=1, device_id=(d, flip(l, j)), device_id_type=MESH)
    for p in planes[1:]:
        pl.semaphore_signal(barrier, inc=1, device_id=(p, l), device_id_type=MESH)
    pl.semaphore_wait(barrier, n_label - 1 + n_dp - 1)

    def copy(g, part, send, recv, to):
        return pltpu.make_async_remote_copy(
            src_ref=blk_ref.at[g, part], dst_ref=blk_ref.at[g, part], send_sem=send,
            recv_sem=recv, device_id=to, device_id_type=MESH,
        )

    def z_copy(s):
        g = planes[s] * n_label + l
        onward = jnp.where(planes[s] < d, d + 1, d - 1)
        to = outward if s == 0 else jnp.minimum(onward, n_dp - 1)
        return copy(g, whole, z_sem.at[s], recv_sem.at[g], (to, l))

    def z_first():
        g = d * n_label + l
        return copy(g, whole, z_sem.at[n_dp], recv_sem.at[g], (toward, l))

    def arrived(g, part, sem):
        copy(g, part, z_sem.at[0], sem, (d, sib)).wait_recv()

    def sends(s):
        base = planes[s] * n_label
        own, gx, gy, gd = base + l, base + xn, base + yn, base + diag
        sem = [send_sem.at[s * 8 + i] for i in range(8)]
        if s == 1:
            ux, uy, ud = (d * n_label + k for k in (xn, yn, diag))
            return [
                (ux, whole, sem[0], recv_sem.at[ux], (near, l)),
                (uy, whole, sem[1], recv_sem.at[uy], (near, l)),
                (own, whole, sem[2], recv_sem.at[own], (d, sib)),
                (ud, whole, sem[3], recv_sem.at[ud], (near, l)),
                (gx, whole, sem[4], recv_sem.at[gx], (d, sib)),
                (gy, whole, sem[6], recv_sem.at[gy], (d, sib)),
                (gd, whole, sem[7], recv_sem.at[gd], (d, sib)),
            ]
        return [
            (own, whole, sem[0], recv_sem.at[own], (d, xn)),
            (own, whole, sem[1], recv_sem.at[own], (d, yn)),
            (own, whole, sem[2], recv_sem.at[own], (d, sib)),
            (gx, first, sem[3], recv_sem.at[gx], (d, yn)),
            (gx, whole, sem[4], recv_sem.at[gx], (d, sib)),
            (gy, second, sem[5], half_sem.at[planes[s]], (d, xn)),
            (gy, whole, sem[6], recv_sem.at[gy], (d, sib)),
            (gd, whole, sem[7], recv_sem.at[gd], (d, sib)),
        ]

    def stage_a(s):
        g = planes[s] * n_label + l
        if s > 0:
            arrived(g, whole, recv_sem.at[g])
        else:
            z_first().start()

        @pl.when(inner)
        def _():
            z_copy(s).start()

        for c in sends(s)[2 if s == 1 else 0:3]:
            copy(*c).start()

    def stage_b(s):
        gx, gy = planes[s] * n_label + xn, planes[s] * n_label + yn
        arrived(gx, whole, recv_sem.at[gx])
        for c in sends(s)[4 if s == 1 else 3:5]:
            copy(*c).start()
        arrived(gy, whole, recv_sem.at[gy])
        for c in sends(s)[5:6 if s == 1 else 7]:
            copy(*c).start()

    def stage_c(s):
        g = planes[s] * n_label + diag
        arrived(g, whole if s == 1 else first, recv_sem.at[g])
        if s != 1:
            arrived(g, second, half_sem.at[planes[s]])
        copy(*sends(s)[-1]).start()

    def send_near():
        for i in (0, 1, 3):
            copy(*sends(1)[i]).start()

    def stage_d(s):
        for j in (1, 3, 5, 7):
            g = planes[s] * n_label + flip(l, j)
            arrived(g, whole, recv_sem.at[g])

    def gather_own(start, stop, stride):
        @pl.loop(0, (stop - start + stride - 1) // stride)
        def _(i):
            j = start + i * stride
            for h in range(chunks):
                pick = gather_chunk(
                    blk_ref, d * n_label + flip(l, j), j, l * clus_dev + h * CHUNK, h * CHUNK,
                    beam, x_ref, off_ref,
                )
                pick_ref[j, h * rows:(h + 1) * rows, :] = pick

    def signals(start, stop):
        @pl.loop(start // 4, stop // 4)
        def _(c2):
            for u in range(4):
                c = c2 * 4 + u
                w = w_ref[c]
                sig = signal_of(x_ref[c], off_ref[c], w, n_pos)
                sig_ref[c] = sig
                y_ref[c] = jnp.dot(sig, w, preferred_element_type=jnp.float32).astype(jnp.bfloat16)

    def grad_copy(j):
        slot = (j - 1) // 2 if j % 2 else 4 + j // 2
        to = sib if j % 2 else flip(l, j)
        return pltpu.make_async_remote_copy(
            src_ref=part_ref.at[j], dst_ref=back_ref.at[slot], send_sem=back_send.at[j],
            recv_sem=back_recv.at[slot], device_id=(d, to), device_id_type=MESH,
        )

    def part_of(j):
        y = y_ref[:, j * SLOTS:(j + 1) * SLOTS, :].reshape(clus_dev * SLOTS, y_ref.shape[2])
        return tn_dot(pick_ref[j], y)

    quarter = clus_dev // 4
    load_q.wait()
    stage_a(0)
    gather_own(0, 1, 1)
    stage_b(0)
    stage_a(1)
    gather_own(2, 5, 2)
    stage_c(0)
    stage_a(2)
    gather_own(6, 7, 1)
    stage_d(0)
    gather_own(1, 4, 2)
    stage_a(3)
    send_near()
    gather_own(5, 8, 2)
    stage_b(2)
    load_w.wait()
    signals(0, quarter)
    stage_c(2)
    stage_b(3)
    signals(quarter, 2 * quarter)
    stage_b(1)
    signals(2 * quarter, 3 * quarter)
    stage_c(3)
    stage_c(1)
    signals(3 * quarter, clus_dev)
    for j in (7, 3, 5, 1):
        part_ref[j] = part_of(j).astype(jnp.bfloat16)
        grad_copy(j).start()
    for j in (6, 2, 4, 0):
        value = part_of(j)
        grad_copy(j + 1).wait_recv()
        value = value + back_ref[j // 2].astype(jnp.float32)
        if j:
            part_ref[j] = value.astype(jnp.bfloat16)
            grad_copy(j).start()
        else:
            grad_ref[...] = value

    @pl.loop(0, CHUNK)
    def _(c):
        at = d * CHUNK + c
        new_ref[c] = w_ref[at].astype(jnp.float32) - STEP_SIZE * tn_dot(sig_ref[at], x_ref[at])

    for s in range(1, n_dp):
        stage_d(s)

        @pl.loop(0, n_label // 4)
        def _(i):
            for u in range(4):
                j = i * 4 + u
                gather_chunk(
                    blk_ref, planes[s] * n_label + j, j, l * clus_dev + d * CHUNK, 0, beam,
                    x_ref, off_ref,
                )

        @pl.loop(0, CHUNK // 4)
        def _(c2):
            for u in range(4):
                c = c2 * 4 + u
                x = x_ref[c]
                sig = signal_of(x, off_ref[c], w_ref[d * CHUNK + c], n_pos)
                new_ref[c] = new_ref[c] - STEP_SIZE * tn_dot(sig, x)

    total = grad_ref[...]
    for j in (2, 4, 6):
        grad_copy(j).wait_recv()
        total = total + back_ref[4 + j // 2].astype(jnp.float32)
    grad_ref[...] = total
    for j in range(1, n_label):
        grad_copy(j).wait_send()
    z_first().wait_send()

    @pl.when(inner)
    def _():
        for s in range(n_dp):
            z_copy(s).wait_send()

    for s in range(n_dp):
        for c in sends(s):
            copy(*c).wait_send()


def make_block(queries, beams, positive_slots, owner, cluster_size):
    q_dev, width = queries.shape
    beam, n_pos = beams.shape[1], positive_slots.shape[1]
    ids = jnp.arange(owner.shape[0], dtype=jnp.int32)
    lookup = beams[:, :, None] == ids[None, None, :]
    slot = jnp.sum(jnp.where(lookup, owner[None, None, :], 0), axis=2)
    where_p = positive_slots[:, :, None] // cluster_size == jnp.arange(beam, dtype=jnp.int32)
    pos_slot = jnp.sum(jnp.where(where_p, slot[:, None, :], 0), axis=2)
    pos_label = positive_slots % cluster_size
    meta = jnp.concatenate(
        [
            jnp.pad(pos_slot, ((0, 0), (0, 16 - n_pos))),
            jnp.pad(pos_label, ((0, 0), (0, 16 - n_pos))),
            jnp.pad(slot, ((0, 0), (0, 32 - beam)), constant_values=-1),
        ],
        axis=1,
    )
    tiles = queries.reshape(q_dev, width // q_dev, q_dev).transpose(1, 0, 2).reshape(width, q_dev)
    return jnp.concatenate([tiles, meta.T.astype(jnp.bfloat16)], axis=0)


def sparse_body(queries, beams, positive_slots, owner, label_weight):
    n_label = lax.axis_size("label")
    n_dp = lax.axis_size("dp")
    q_dev, width = queries.shape
    clus_dev = owner.shape[0] // n_label
    cluster_size = label_weight.shape[0] // clus_dev
    block = make_block(queries, beams, positive_slots, owner, cluster_size)
    slots = n_label * SLOTS
    length = block.shape[0]
    grad, new = pl.pallas_call(
        functools.partial(step_kernel, n_dp, n_label, beams.shape[1], positive_slots.shape[1]),
        out_shape=(
            jax.ShapeDtypeStruct((q_dev, width), jnp.float32),
            jax.ShapeDtypeStruct((CHUNK, cluster_size, width), jnp.float32),
        ),
        in_specs=[pl.BlockSpec(memory_space=pl.ANY)] * 2,
        out_specs=(pl.BlockSpec(memory_space=pltpu.VMEM),) * 2,
        scratch_shapes=[
            pltpu.VMEM((n_dp * n_label, length, q_dev), jnp.bfloat16),
            pltpu.VMEM((clus_dev, cluster_size, width), jnp.bfloat16),
            pltpu.VMEM((clus_dev, slots, width), jnp.bfloat16),
            pltpu.VMEM((clus_dev, slots, width), jnp.bfloat16),
            pltpu.VMEM((n_label, clus_dev * SLOTS, q_dev), jnp.bfloat16),
            pltpu.VMEM((clus_dev, slots, 16), jnp.float32),
            pltpu.VMEM((clus_dev, slots, cluster_size), jnp.bfloat16),
            pltpu.VMEM((n_label, q_dev, width), jnp.bfloat16),
            pltpu.VMEM((n_label, q_dev, width), jnp.bfloat16),
            pltpu.SemaphoreType.DMA((2,)),
            pltpu.SemaphoreType.DMA((n_dp * n_label,)),
            pltpu.SemaphoreType.DMA((n_dp,)),
            pltpu.SemaphoreType.DMA((n_dp + 1,)),
            pltpu.SemaphoreType.DMA((8 * n_dp,)),
            pltpu.SemaphoreType.DMA((n_label,)),
            pltpu.SemaphoreType.DMA((n_label,)),
        ],
        compiler_params=pltpu.CompilerParams(
            vmem_limit_bytes=58 << 20, collective_id=0, has_side_effects=True
        ),
    )(block, label_weight.reshape(clus_dev, cluster_size, width))
    return (grad, new.reshape(CHUNK * cluster_size, width))


def choose(queries, beams, positive_slots, owner, label_weight):
    n_dp, n_label = lax.axis_size("dp"), lax.axis_size("label")
    q_dev, width = queries.shape
    fits = n_dp == 4 and n_label == 8 and queries.size * n_dp * n_label * 2 <= (8 << 20) and n_label * SLOTS == q_dev
    fits = fits and q_dev == 128 and width % q_dev == 0 and beams.shape[1] <= 32
    fits = fits and owner.shape[0] == n_label * n_dp * CHUNK and positive_slots.shape[1] <= 16
    fits = fits and max(2, q_dev * 3 // 32) <= SLOTS and owner.shape[0] <= 256
    form = sparse_body if fits else body
    return form(queries, beams, positive_slots, owner, label_weight)


def solution(mesh):
    in_specs = (
        P(("dp", "label"), None),
        P(("dp", "label"), None),
        P(("dp", "label"), None),
        P(),
        P("label", None),
    )
    out_specs = (P(("dp", "label"), None), P(("label", "dp"), None))
    return jax.shard_map(
        choose, mesh=mesh, in_specs=in_specs, out_specs=out_specs, check_vma=False
    )
```

```python
import functools

import jax
import jax.numpy as jnp
from jax import lax
from jax.experimental import pallas as pl
from jax.experimental.pallas import tpu as pltpu
from jax.sharding import PartitionSpec as P

STEP_SIZE = 0.02


def slot_table(keys, count, most):
    q_rows, beam = keys.shape
    pairs = q_rows * beam
    ids = jnp.arange(count, dtype=jnp.int32)
    member = jnp.any(keys[:, :, None] == ids[None, None, :], axis=1).astype(jnp.float32)
    row_ids = jnp.arange(q_rows, dtype=jnp.int32)
    lower = (row_ids[:, None] > row_ids[None, :]).astype(jnp.float32)
    before = jnp.dot(lower, member, precision=lax.Precision.HIGHEST)
    safe_keys = jnp.minimum(keys, count - 1)
    rank = jnp.take_along_axis(before, safe_keys, axis=1).astype(jnp.int32)
    flat_keys = keys.reshape(pairs)
    target = jnp.where(flat_keys < count, flat_keys * most + rank.reshape(pairs), count * most)
    table = (
        jnp.full((count * most,), pairs, jnp.int32)
        .at[target]
        .set(jnp.arange(pairs, dtype=jnp.int32), mode="drop")
    )
    return (target, table)


def body(queries, beams, positive_slots, owner, label_weight):
    n_label = lax.axis_size("label")
    q_dev, width = queries.shape
    beam = beams.shape[1]
    n_pos = positive_slots.shape[1]
    clusters = owner.shape[0]
    clus_dev = clusters // n_label
    cluster_size = label_weight.shape[0] // clus_dev
    most = max(2, q_dev * 3 // 32)
    pairs = q_dev * beam
    rows_dev = clus_dev * most
    lookup = beams[:, :, None] == jnp.arange(clusters, dtype=jnp.int32)[None, None, :]
    pair_slot = jnp.sum(jnp.where(lookup, owner[None, None, :], 0), axis=2)
    position = jnp.arange(beam, dtype=jnp.int32)
    inside = positive_slots[:, None, :] // cluster_size == position[None, :, None]
    pair_offset = jnp.where(inside, positive_slots[:, None, :] % cluster_size, -1)
    target, table = slot_table(pair_slot, clusters, most)
    filled = table < pairs
    padded = jnp.concatenate([queries, jnp.zeros((1, width), queries.dtype)], axis=0)
    send_q = padded[jnp.where(filled, table // beam, q_dev)]
    flat_off = pair_offset.reshape(pairs, n_pos)
    send_off = jnp.where(filled[:, None], flat_off[jnp.where(filled, table, 0)], -1)
    moved = (
        lax.all_to_all(
            send_q.reshape(n_label, rows_dev, width),
            "label",
            split_axis=0,
            concat_axis=0,
            tiled=True,
        ),
        lax.all_to_all(
            send_off.astype(jnp.bfloat16).reshape(n_label, rows_dev, n_pos),
            "label",
            split_axis=0,
            concat_axis=0,
            tiled=True,
        ),
        lax.all_to_all(
            filled.astype(jnp.bfloat16).reshape(n_label, rows_dev),
            "label",
            split_axis=0,
            concat_axis=0,
            tiled=True,
        ),
    )
    recv_q = moved[0]
    recv_off = moved[1].astype(jnp.int32)
    recv_fill = moved[2].astype(jnp.float32)
    incoming = n_label * most
    recv_q = (
        recv_q.reshape(n_label, clus_dev, most, width)
        .transpose(1, 0, 2, 3)
        .reshape(clus_dev, incoming, width)
    )
    recv_off = (
        recv_off.reshape(n_label, clus_dev, most, n_pos)
        .transpose(1, 0, 2, 3)
        .reshape(clus_dev, incoming, n_pos)
    )
    recv_fill = (
        recv_fill.reshape(n_label, clus_dev, most).transpose(1, 0, 2).reshape(clus_dev, incoming)
    )
    weights = label_weight.reshape(clus_dev, cluster_size, width)
    scores = jnp.einsum("cnd,cld->cnl", recv_q, weights, preferred_element_type=jnp.float32)
    labels = jnp.arange(cluster_size, dtype=jnp.int32)
    positive = jnp.any(recv_off[..., None] == labels, axis=-2).astype(jnp.float32)
    signal = ((jax.nn.sigmoid(scores) - positive) * recv_fill[..., None]).astype(jnp.bfloat16)
    signal_split = signal.reshape(clus_dev, n_label, most, cluster_size)
    part_dq = jnp.einsum(
        "csml,cld->scmd", signal_split, weights, preferred_element_type=jnp.float32
    ).astype(jnp.bfloat16)
    part_dw = jnp.einsum("cnl,cnd->cld", signal, recv_q, preferred_element_type=jnp.float32)
    part_dw = part_dw.reshape(clus_dev * cluster_size, width)
    back = lax.all_to_all(
        part_dq.reshape(n_label, rows_dev, width), "label", split_axis=0, concat_axis=0, tiled=True
    )
    back_rows = back.reshape(clusters * most, width)[target]
    query_grad = jnp.sum(back_rows.reshape(q_dev, beam, width).astype(jnp.float32), axis=1)
    summed = lax.psum_scatter(part_dw, "dp", scatter_dimension=0, tiled=True)
    share = summed.shape[0]
    own_rows = lax.dynamic_slice_in_dim(
        label_weight, lax.axis_index("dp") * share, share, 0
    ).astype(jnp.float32)
    return (query_grad, own_rows - STEP_SIZE * summed)


MESH = pl.DeviceIdType.MESH
SLOTS = 16
CHUNK = 8


def tn_dot(a, b):
    return lax.dot_general(a, b, (((0,), (0,)), ((), ())), preferred_element_type=jnp.float32)


def nt_dot(a, b):
    return lax.dot_general(a, b, (((1,), (1,)), ((), ())), preferred_element_type=jnp.float32)


def pick_matrix(meta, beam, first):
    q_dev = meta.shape[1]
    ids = (first + lax.broadcasted_iota(jnp.int32, (CHUNK, q_dev), 0)).astype(jnp.float32)
    member = meta[32:33, :] == ids
    for j in range(1, beam):
        member = member | (meta[32 + j:33 + j, :] == ids)
    member = member.astype(jnp.float32)
    row = lax.broadcasted_iota(jnp.int32, (q_dev, q_dev), 0)
    col = lax.broadcasted_iota(jnp.int32, (q_dev, q_dev), 1)
    upper = (row < col).astype(jnp.float32).astype(jnp.bfloat16)
    rank = jnp.dot(member.astype(jnp.bfloat16), upper, preferred_element_type=jnp.float32)
    code = jnp.where(member > 0, rank, -1.0)
    wide = jnp.broadcast_to(code[:, None, :], (CHUNK, SLOTS, q_dev))
    place = lax.broadcasted_iota(jnp.int32, (CHUNK, SLOTS, q_dev), 1).astype(jnp.float32)
    pick = (wide == place).astype(jnp.float32).reshape(CHUNK * SLOTS, q_dev)
    return pick.astype(jnp.bfloat16)


def gather_chunk(blk_ref, src, b, first, at, beam, x_ref, off_ref):
    q_dev = blk_ref.shape[2]
    tiles = (blk_ref.shape[1] - 64) // q_dev
    meta = blk_ref[src, tiles * q_dev:tiles * q_dev + 64, :]
    pick = pick_matrix(meta.astype(jnp.float32), beam, first)
    q = jnp.concatenate([blk_ref[src, k * q_dev:(k + 1) * q_dev, :] for k in range(tiles)], axis=1)
    rows = jnp.dot(pick, q, preferred_element_type=jnp.float32).astype(jnp.bfloat16)
    here = pl.ds(pl.multiple_of(b * SLOTS, SLOTS), SLOTS)
    x_ref[pl.ds(at, CHUNK), here, :] = rows.reshape(CHUNK, SLOTS, rows.shape[1])
    high = nt_dot(pick, meta[0:16, :])
    low = nt_dot(pick, meta[16:32, :])
    cluster = first + lax.broadcasted_iota(jnp.int32, high.shape, 0) // SLOTS
    off = jnp.where(high == cluster.astype(jnp.float32), low, -1.0)
    off_ref[pl.ds(at, CHUNK), here, :] = off.reshape(CHUNK, SLOTS, 16)
    return pick


def signal_of(x, off, w, n_pos):
    score = nt_dot(x, w)
    label = lax.broadcasted_iota(jnp.int32, score.shape, 1).astype(jnp.float32)
    hit = off[:, 0:1] == label
    for p in range(1, n_pos):
        hit = hit | (off[:, p:p + 1] == label)
    return (jax.nn.sigmoid(score) - hit.astype(jnp.float32)).astype(jnp.bfloat16)


def flip(l, j):
    return ((l // 4 + j // 4) % 2) * 4 + ((l // 2 + j // 2) % 2) * 2 + (l + j) % 2


def step_kernel(n_dp, n_label, beam, n_pos, mine_ref, w_hbm, grad_ref, new_ref,
                blk_ref, w_ref, x_ref, y_ref, pick_ref, off_ref, sig_ref, part_ref, back_ref,
                local_sem, recv_sem, half_sem, z_sem, send_sem, back_send, back_recv):
    d, l = lax.axis_index("dp"), lax.axis_index("label")
    clus_dev = w_ref.shape[0]
    chunks = clus_dev // CHUNK
    rows = CHUNK * SLOTS
    length = blk_ref.shape[1]
    half = length // 2
    xn, yn, sib, diag = flip(l, 2), flip(l, 4), flip(l, 1), flip(l, 6)
    whole, first, second = pl.ds(0, length), pl.ds(0, half), pl.ds(half, half)
    near = jnp.where(d == 0, 1, jnp.where(d == 1, 0, jnp.where(d == 2, 3, 2)))
    mid = jnp.where(d == 0, 2, jnp.where(d == 1, 2, 1))
    far = jnp.where(d < 2, 3, 0)
    planes = [d, near, mid, far]
    inner = (d == 1) | (d == 2)
    toward = jnp.where(d < 2, d + 1, d - 1)
    outward = jnp.where(d == 1, 0, 3)

    load_w = pltpu.make_async_copy(w_hbm, w_ref, local_sem.at[0])
    load_w.start()
    load_q = pltpu.make_async_copy(mine_ref, blk_ref.at[d * n_label + l], local_sem.at[1])
    load_q.start()

    barrier = pltpu.get_barrier_semaphore()
    for j in range(1, n_label):
        pl.semaphore_signal(barrier, inc=1, device_id=(d, flip(l, j)), device_id_type=MESH)
    for p in planes[1:]:
        pl.semaphore_signal(barrier, inc=1, device_id=(p, l), device_id_type=MESH)
    pl.semaphore_wait(barrier, n_label - 1 + n_dp - 1)

    def copy(g, part, send, recv, to):
        return pltpu.make_async_remote_copy(
            src_ref=blk_ref.at[g, part], dst_ref=blk_ref.at[g, part], send_sem=send,
            recv_sem=recv, device_id=to, device_id_type=MESH,
        )

    def z_copy(s):
        g = planes[s] * n_label + l
        onward = jnp.where(planes[s] < d, d + 1, d - 1)
        to = outward if s == 0 else jnp.minimum(onward, n_dp - 1)
        return copy(g, whole, z_sem.at[s], recv_sem.at[g], (to, l))

    def z_first():
        g = d * n_label + l
        return copy(g, whole, z_sem.at[n_dp], recv_sem.at[g], (toward, l))

    def arrived(g, part, sem):
        copy(g, part, z_sem.at[0], sem, (d, sib)).wait_recv()

    def sends(s):
        base = planes[s] * n_label
        own, gx, gy, gd = base + l, base + xn, base + yn, base + diag
        sem = [send_sem.at[s * 8 + i] for i in range(8)]
        if s == 1:
            ux, uy, ud = (d * n_label + k for k in (xn, yn, diag))
            return [
                (ux, whole, sem[0], recv_sem.at[ux], (near, l)),
                (uy, whole, sem[1], recv_sem.at[uy], (near, l)),
                (own, whole, sem[2], recv_sem.at[own], (d, sib)),
                (ud, whole, sem[3], recv_sem.at[ud], (near, l)),
                (gx, whole, sem[4], recv_sem.at[gx], (d, sib)),
                (gy, whole, sem[6], recv_sem.at[gy], (d, sib)),
                (gd, whole, sem[7], recv_sem.at[gd], (d, sib)),
            ]
        return [
            (own, whole, sem[0], recv_sem.at[own], (d, xn)),
            (own, whole, sem[1], recv_sem.at[own], (d, yn)),
            (own, whole, sem[2], recv_sem.at[own], (d, sib)),
            (gx, first, sem[3], recv_sem.at[gx], (d, yn)),
            (gx, whole, sem[4], recv_sem.at[gx], (d, sib)),
            (gy, second, sem[5], half_sem.at[planes[s]], (d, xn)),
            (gy, whole, sem[6], recv_sem.at[gy], (d, sib)),
            (gd, whole, sem[7], recv_sem.at[gd], (d, sib)),
        ]

    def stage_a(s):
        g = planes[s] * n_label + l
        if s > 0:
            arrived(g, whole, recv_sem.at[g])
        else:
            z_first().start()

        @pl.when(inner)
        def _():
            z_copy(s).start()

        for c in sends(s)[2 if s == 1 else 0:3]:
            copy(*c).start()

    def stage_b(s):
        gx, gy = planes[s] * n_label + xn, planes[s] * n_label + yn
        arrived(gx, whole, recv_sem.at[gx])
        for c in sends(s)[4 if s == 1 else 3:5]:
            copy(*c).start()
        arrived(gy, whole, recv_sem.at[gy])
        for c in sends(s)[5:6 if s == 1 else 7]:
            copy(*c).start()

    def stage_c(s):
        g = planes[s] * n_label + diag
        arrived(g, whole if s == 1 else first, recv_sem.at[g])
        if s != 1:
            arrived(g, second, half_sem.at[planes[s]])
        copy(*sends(s)[-1]).start()

    def send_near():
        for i in (0, 1, 3):
            copy(*sends(1)[i]).start()

    def stage_d(s):
        for j in (1, 3, 5, 7):
            g = planes[s] * n_label + flip(l, j)
            arrived(g, whole, recv_sem.at[g])

    def gather_own(start, stop, stride):
        @pl.loop(0, (stop - start + stride - 1) // stride)
        def _(i):
            j = start + i * stride
            for h in range(chunks):
                pick = gather_chunk(
                    blk_ref, d * n_label + flip(l, j), j, l * clus_dev + h * CHUNK, h * CHUNK,
                    beam, x_ref, off_ref,
                )
                pick_ref[j, h * rows:(h + 1) * rows, :] = pick

    def signals(start, stop):
        @pl.loop(start // 4, stop // 4)
        def _(c2):
            for u in range(4):
                c = c2 * 4 + u
                w = w_ref[c]
                sig = signal_of(x_ref[c], off_ref[c], w, n_pos)
                sig_ref[c] = sig
                y_ref[c] = jnp.dot(sig, w, preferred_element_type=jnp.float32).astype(jnp.bfloat16)

    def grad_copy(j):
        slot = (j - 1) // 2 if j % 2 else 4 + j // 2
        to = sib if j % 2 else flip(l, j)
        return pltpu.make_async_remote_copy(
            src_ref=part_ref.at[j], dst_ref=back_ref.at[slot], send_sem=back_send.at[j],
            recv_sem=back_recv.at[slot], device_id=(d, to), device_id_type=MESH,
        )

    def part_of(j):
        y = y_ref[:, j * SLOTS:(j + 1) * SLOTS, :].reshape(clus_dev * SLOTS, y_ref.shape[2])
        return tn_dot(pick_ref[j], y)

    quarter = clus_dev // 4
    load_q.wait()
    stage_a(0)
    gather_own(0, 1, 1)
    stage_b(0)
    stage_a(1)
    gather_own(2, 5, 2)
    stage_c(0)
    stage_a(2)
    gather_own(6, 7, 1)
    stage_d(0)
    gather_own(1, 4, 2)
    stage_a(3)
    send_near()
    gather_own(5, 8, 2)
    stage_b(2)
    load_w.wait()
    signals(0, quarter)
    stage_c(2)
    stage_b(3)
    signals(quarter, 2 * quarter)
    stage_b(1)
    signals(2 * quarter, 3 * quarter)
    stage_c(3)
    stage_c(1)
    signals(3 * quarter, clus_dev)
    for j in (7, 3, 5, 1):
        part_ref[j] = part_of(j).astype(jnp.bfloat16)
        grad_copy(j).start()
    for j in (6, 2, 4, 0):
        value = part_of(j)
        grad_copy(j + 1).wait_recv()
        value = value + back_ref[j // 2].astype(jnp.float32)
        if j:
            part_ref[j] = value.astype(jnp.bfloat16)
            grad_copy(j).start()
        else:
            grad_ref[...] = value

    @pl.loop(0, CHUNK)
    def _(c):
        at = d * CHUNK + c
        new_ref[c] = w_ref[at].astype(jnp.float32) - STEP_SIZE * tn_dot(sig_ref[at], x_ref[at])

    for s in (2, 3, 1):
        stage_d(s)

        @pl.loop(0, n_label // 8)
        def _(i):
            for u in range(8):
                j = i * 8 + u
                gather_chunk(
                    blk_ref, planes[s] * n_label + j, j, l * clus_dev + d * CHUNK, 0, beam,
                    x_ref, off_ref,
                )

        @pl.loop(0, CHUNK // 8)
        def _(c2):
            for u in range(8):
                c = c2 * 8 + u
                x = x_ref[c]
                sig = signal_of(x, off_ref[c], w_ref[d * CHUNK + c], n_pos)
                new_ref[c] = new_ref[c] - STEP_SIZE * tn_dot(sig, x)

    total = grad_ref[...]
    for j in (2, 4, 6):
        grad_copy(j).wait_recv()
        total = total + back_ref[4 + j // 2].astype(jnp.float32)
    grad_ref[...] = total
    for j in range(1, n_label):
        grad_copy(j).wait_send()
    z_first().wait_send()

    @pl.when(inner)
    def _():
        for s in range(n_dp):
            z_copy(s).wait_send()

    for s in range(n_dp):
        for c in sends(s):
            copy(*c).wait_send()


def make_block(queries, beams, positive_slots, owner, cluster_size):
    q_dev, width = queries.shape
    beam, n_pos = beams.shape[1], positive_slots.shape[1]
    ids = jnp.arange(owner.shape[0], dtype=jnp.int32)
    lookup = beams[:, :, None] == ids[None, None, :]
    slot = jnp.sum(jnp.where(lookup, owner[None, None, :], 0), axis=2)
    where_p = positive_slots[:, :, None] // cluster_size == jnp.arange(beam, dtype=jnp.int32)
    pos_slot = jnp.sum(jnp.where(where_p, slot[:, None, :], 0), axis=2)
    pos_label = positive_slots % cluster_size
    meta = jnp.concatenate(
        [
            jnp.pad(pos_slot, ((0, 0), (0, 16 - n_pos))),
            jnp.pad(pos_label, ((0, 0), (0, 16 - n_pos))),
            jnp.pad(slot, ((0, 0), (0, 32 - beam)), constant_values=-1),
        ],
        axis=1,
    )
    tiles = queries.reshape(q_dev, width // q_dev, q_dev).transpose(1, 0, 2).reshape(width, q_dev)
    return jnp.concatenate([tiles, meta.T.astype(jnp.bfloat16)], axis=0)


def sparse_body(queries, beams, positive_slots, owner, label_weight):
    n_label = lax.axis_size("label")
    n_dp = lax.axis_size("dp")
    q_dev, width = queries.shape
    clus_dev = owner.shape[0] // n_label
    cluster_size = label_weight.shape[0] // clus_dev
    block = make_block(queries, beams, positive_slots, owner, cluster_size)
    slots = n_label * SLOTS
    length = block.shape[0]
    grad, new = pl.pallas_call(
        functools.partial(step_kernel, n_dp, n_label, beams.shape[1], positive_slots.shape[1]),
        out_shape=(
            jax.ShapeDtypeStruct((q_dev, width), jnp.float32),
            jax.ShapeDtypeStruct((CHUNK, cluster_size, width), jnp.float32),
        ),
        in_specs=[pl.BlockSpec(memory_space=pl.ANY)] * 2,
        out_specs=(pl.BlockSpec(memory_space=pltpu.VMEM),) * 2,
        scratch_shapes=[
            pltpu.VMEM((n_dp * n_label, length, q_dev), jnp.bfloat16),
            pltpu.VMEM((clus_dev, cluster_size, width), jnp.bfloat16),
            pltpu.VMEM((clus_dev, slots, width), jnp.bfloat16),
            pltpu.VMEM((clus_dev, slots, width), jnp.bfloat16),
            pltpu.VMEM((n_label, clus_dev * SLOTS, q_dev), jnp.bfloat16),
            pltpu.VMEM((clus_dev, slots, 16), jnp.float32),
            pltpu.VMEM((clus_dev, slots, cluster_size), jnp.bfloat16),
            pltpu.VMEM((n_label, q_dev, width), jnp.bfloat16),
            pltpu.VMEM((n_label, q_dev, width), jnp.bfloat16),
            pltpu.SemaphoreType.DMA((2,)),
            pltpu.SemaphoreType.DMA((n_dp * n_label,)),
            pltpu.SemaphoreType.DMA((n_dp,)),
            pltpu.SemaphoreType.DMA((n_dp + 1,)),
            pltpu.SemaphoreType.DMA((8 * n_dp,)),
            pltpu.SemaphoreType.DMA((n_label,)),
            pltpu.SemaphoreType.DMA((n_label,)),
        ],
        compiler_params=pltpu.CompilerParams(
            vmem_limit_bytes=58 << 20, collective_id=0, has_side_effects=True
        ),
    )(block, label_weight.reshape(clus_dev, cluster_size, width))
    return (grad, new.reshape(CHUNK * cluster_size, width))


def choose(queries, beams, positive_slots, owner, label_weight):
    n_dp, n_label = lax.axis_size("dp"), lax.axis_size("label")
    q_dev, width = queries.shape
    fits = n_dp == 4 and n_label == 8 and queries.size * n_dp * n_label * 2 <= (8 << 20) and n_label * SLOTS == q_dev
    fits = fits and q_dev == 128 and width % q_dev == 0 and beams.shape[1] <= 32
    fits = fits and owner.shape[0] == n_label * n_dp * CHUNK and positive_slots.shape[1] <= 16
    fits = fits and max(2, q_dev * 3 // 32) <= SLOTS and owner.shape[0] <= 256
    form = sparse_body if fits else body
    return form(queries, beams, positive_slots, owner, label_weight)


def solution(mesh):
    in_specs = (
        P(("dp", "label"), None),
        P(("dp", "label"), None),
        P(("dp", "label"), None),
        P(),
        P("label", None),
    )
    out_specs = (P(("dp", "label"), None), P(("label", "dp"), None))
    return jax.shard_map(
        choose, mesh=mesh, in_specs=in_specs, out_specs=out_specs, check_vma=False
    )
```
